256 devices in a mesh: band: 8 (over x_lo, y), slab: 32 (over x_hi, z, core).
Axes of the slice: x: 4 (x_hi: 2, x_lo: 2; x = x_hi * 2 + x_lo), y: 4, z: 8, core: 2. Of those that a mesh axis runs over, the one named last changes fastest.
Arguments:
- resident: float32 [8, 192, 192, 192], P('band', 'slab'), may hold values from -6 to 6
- owned: float32 [8, 4, 192, 192, 192], P('band', None, 'slab'), may hold values from -6 to 6
- owner: int32 [2], replicated, may hold values from 0 to 7, as said below
Outputs:
- exchange: float32 [8, 192, 192, 192], P('band', 'slab')
The draws below stay inside these ranges and needn't reach their ends.
Inputs may be any that keep to these rules, and one draw needn't show every extreme that they name: The owner groups of the 2 rounds are distinct, and group 7 owns one of the rounds.
All inputs are finite; a program needn't handle non-finite values.
Results may differ from the reference program's by a relative error of at most 0.0001.
Values sent between devices are 32-bit elements; how exact they have to be, the bound alone decides.
No kernel may reach another device: no remote copies, remote signals or barrier semaphores. Data moves between devices by JAX's collectives and lax.ppermute only.
A program may use at most 128 MiB of HBM per device.

```python
import math
import jax
import jax.numpy as jnp
from jax import lax

N = 192
NB = 4
ROUNDS = 2
GROUPS = 8


def draw_owner(key, part):
    key = jax.random.fold_in(key, 11)
    score_key = jax.random.fold_in(key, 1)
    order_key = jax.random.fold_in(key, 2)
    scores = jax.random.randint(score_key, (GROUPS - 1,), 0, 1 << 20, dtype=jnp.int32)
    scores = scores * GROUPS + jnp.arange(GROUPS - 1, dtype=jnp.int32)
    others = jnp.argsort(scores, stable=True)[:ROUNDS - 1].astype(jnp.int32)
    chosen = jnp.concatenate([others, jnp.full((1,), GROUPS - 1, jnp.int32)])
    return jax.random.permutation(order_key, chosen).astype(jnp.int32)


def block_scale(own_key, shape, split, smallest, top_value):
    loudness = 1.0
    for position, shards_of in split:
        draws = jax.random.uniform(jax.random.fold_in(jax.random.fold_in(own_key, 6), position), (shards_of,), jnp.float32, smallest / len(split), top_value / len(split))
        loudness = loudness * jnp.repeat(jnp.exp(draws), shape[position] // shards_of).reshape((-1,) + (1,) * (len(shape) - 1 - position))
    return loudness


def centred(rng, shape, spread, limit, cuts=(), held_as=jnp.bfloat16):
    entries = jax.random.normal(rng, shape, jnp.float32) * spread
    if len(cuts) > 0:
        entries = block_scale(rng, shape, cuts, -0.22, 0.18) * entries
    return jnp.clip(entries, min=-limit, max=limit).astype(held_as)


def setup_inputs(seed: int = 0) -> dict:
    streams_of = jax.random.split(jax.random.key(seed), 4)
    return {
        "resident": centred(streams_of[0], (GROUPS, N, N, N), 1.0, 6.0, ((0, 8), (1, 32)), jnp.float32),
        "owned": centred(streams_of[1], (GROUPS, NB, N, N, N), 1.0, 6.0, ((0, 8), (2, 32)), jnp.float32),
        "owner": draw_owner(jax.random.fold_in(streams_of[3], 71), 0),
    }


highest = lax.Precision.HIGHEST

def cas_matrix(size):
    index = jnp.arange(size, dtype=jnp.int32)
    products = index[:, None] * index[None, :] % size
    phases = products.astype(jnp.float32) * (2.0 * math.pi / size)
    return jnp.cos(phases) + jnp.sin(phases)

def wavenumber(index, size):
    folded = jnp.minimum(index, size - index)
    return folded.astype(jnp.float32) * (2.0 * math.pi / size)

def coulomb_grid(size):
    wave = wavenumber(jnp.arange(size, dtype=jnp.int32), size)
    squared = wave[:, None, None] ** 2 + wave[None, :, None] ** 2 + wave[None, None, :] ** 2
    screen = (4.0 * math.pi / size) ** 2
    return 4.0 * math.pi / (squared + screen) / float(size) ** 3

def forward_three(field, cas):
    field = jnp.einsum('abc,cz->abz', field, cas, precision=highest)
    field = jnp.einsum('abc,by->ayc', field, cas, precision=highest)
    return jnp.einsum('abc,ax->xbc', field, cas, precision=highest)

def inverse_three(field, cas):
    field = jnp.einsum('abc,ax->xbc', field, cas, precision=highest)
    field = jnp.einsum('abc,by->ayc', field, cas, precision=highest)
    return jnp.einsum('abc,cz->abz', field, cas, precision=highest)

def reference(resident, owned, owner):
    cas = cas_matrix(N)
    coulomb = coulomb_grid(N)
    prefactor = -1.0 / math.sqrt(N * ROUNDS * NB)

    def one_group(orbital):
        accumulated = jnp.zeros((N, N, N), jnp.float32)
        for turn_index in range(ROUNDS):
            shared_bands = owned[owner[turn_index]]
            weight = float(turn_index + 1)
            for member in range(NB):
                partner = shared_bands[member]
                spectrum = forward_three(orbital * partner, cas)
                potential = inverse_three(coulomb * spectrum, cas)
                accumulated = accumulated + weight * (partner * potential)
        return accumulated * prefactor
    return lax.map(one_group, resident)
```

```python
import math

import jax
import jax.numpy as jnp
import numpy as np
from jax import lax
from jax.sharding import Mesh, PartitionSpec as P

N = 192
PLANE = ("x_lo", "y", "x_hi", "core")
high = lax.Precision.HIGH


def cas_matrix(size):
    index = np.arange(size)
    phases = (index[:, None] * index[None, :] % size) * (2.0 * math.pi / size)
    return (np.cos(phases) + np.sin(phases)).astype(np.float32)


def coulomb_grid(size):
    index = np.arange(size)
    wave = np.minimum(index, size - index) * (2.0 * math.pi / size)
    squared = wave[:, None, None] ** 2 + wave[None, :, None] ** 2 + wave[None, None, :] ** 2
    return squared


def held_order():
    z, x_hi, core, row = np.meshgrid(np.arange(8), np.arange(2), np.arange(2), np.arange(6), indexing="ij")
    return (6 * (x_hi * 16 + z * 2 + core) + row).reshape(-1)


def wavenumber(index):
    folded = jnp.minimum(index, N - index)
    return folded.astype(jnp.float32) * (2.0 * math.pi / N)


def exchange_plane(blocks):
    return lax.all_to_all(blocks, PLANE, 0, 0, tiled=True)


def exchange_z(blocks):
    return lax.all_to_all(blocks, "z", 0, 0, tiled=True)


def to_blocks(planes):
    count = planes.shape[0]
    blocks = planes.reshape(count, 6, 32, 6, N).transpose(2, 0, 1, 3, 4)
    return blocks.reshape(32, count * 54, 128)


def shards(resident, owned, owner):
    cas = jnp.asarray(cas_matrix(N))
    cas_held = jnp.asarray(cas_matrix(N)[:, held_order()])
    place = lax.axis_index(PLANE)
    pair_wave = wavenumber((place % 8) * 24 + jnp.arange(24, dtype=jnp.int32))
    wave = wavenumber(jnp.arange(N, dtype=jnp.int32))
    squared = pair_wave[:, None, None] ** 2 + wave[None, :, None] ** 2 + wave[None, None, :] ** 2
    screen = (4.0 * math.pi / N) ** 2
    coulomb = 4.0 * math.pi / (squared + screen) / float(N) ** 3

    orbital = exchange_z(exchange_plane(to_blocks(resident)).reshape(8, 216, 128))
    orbital = orbital.reshape(N, 6, N)
    accumulated = jnp.zeros((N, 6, N), jnp.float32)
    weights = -1.0 / math.sqrt(N * 8) * jnp.array([1.0, 1.0, 2.0, 2.0], jnp.float32)
    halves = []
    for half in range(2):
        part = owned[0, 2 * half : 2 * half + 2]
        spread = exchange_plane(to_blocks(part)).reshape(8, 4, 2, 6, 6 * N)
        chosen = jnp.take(spread, owner, axis=0, mode="clip")
        chosen = chosen.transpose(0, 2, 1, 3, 4).reshape(4, 24, 6 * N)
        bands = lax.all_gather(chosen, "z", axis=0, tiled=False)
        halves.append(bands.transpose(1, 0, 2, 3).reshape(4, N, 6, N))
    spectra = []
    for bands in halves:
        pairs = orbital[None] * bands
        pairs = jnp.einsum("paic,ck->paik", pairs, cas, precision=high)
        pairs = jnp.einsum("paic,ka->pkic", pairs, cas_held, precision=high)
        spectra.append(exchange_plane(pairs.reshape(32, 24, 6 * N)))
    filtered = []
    for columns in spectra:
        columns = columns.reshape(32, 24, 6, N)
        matrix = cas.reshape(32, 6, N)
        columns = jnp.einsum("sakc,skb->abc", columns, matrix, precision=high)
        columns = columns * coulomb
        columns = jnp.einsum("abc,skb->sakc", columns, matrix, precision=high)
        filtered.append(exchange_plane(columns.reshape(32, 24, 6 * N)))
    for bands, potential in zip(halves, filtered):
        potential = potential.reshape(4, N, 6, N)
        potential = jnp.einsum("pkic,ka->paic", potential, cas_held, precision=high)
        potential = jnp.einsum("paic,ck->paik", potential, cas, precision=high)
        accumulated = accumulated + jnp.sum(weights[:, None, None, None] * bands * potential, axis=0)
    back = exchange_z(accumulated.reshape(8, 216, 128))
    back = exchange_plane(back.reshape(32, 54, 128))
    return back.reshape(32, 6, 6, N).transpose(1, 0, 2, 3).reshape(1, 6, N, N)


def solution(mesh):
    fine = Mesh(mesh.devices.reshape(2, 4, 2, 8, 2), ("x_lo", "y", "x_hi", "z", "core"))
    band, slab = ("x_lo", "y"), ("x_hi", "z", "core")
    return jax.shard_map(
        shards,
        mesh=fine,
        in_specs=(P(band, slab), P(band, None, slab), P()),
        out_specs=P(band, slab),
        check_vma=False,
    )
```

```python
import functools
import math

import jax
import jax.numpy as jnp
import ml_dtypes
import numpy as np
from jax import lax
from jax.experimental import pallas as pl
from jax.experimental.pallas import tpu as pltpu
from jax.sharding import Mesh, PartitionSpec as P

N = 192
LANES = 6 * N
TILES = LANES // 128
PLANE = ("x_lo", "y", "x_hi", "core")
VMEM = 40 * 1024 * 1024


def cas_matrix():
    index = np.arange(N)
    phases = (index[:, None] * index[None, :] % N) * (2.0 * math.pi / N)
    return np.cos(phases) + np.sin(phases)


def held_order():
    z, x_hi, core, row = np.meshgrid(np.arange(8), np.arange(2), np.arange(2), np.arange(6), indexing="ij")
    return (6 * (x_hi * 16 + z * 2 + core) + row).reshape(-1)


def column_order():
    inner, device = np.meshgrid(np.arange(6), np.arange(32), indexing="ij")
    return (6 * device + inner).reshape(-1)


def two_terms(matrix):
    high = matrix.astype(np.float32).astype(ml_dtypes.bfloat16)
    low = (matrix - high.astype(np.float64)).astype(np.float32).astype(ml_dtypes.bfloat16)
    return np.stack([high, low])


def lane_matrices():
    cas = cas_matrix()
    even, odd = np.zeros((256, 256)), np.zeros((256, 256))
    even[:N, :N] = cas
    odd[64:, 64:128] = cas[:, 128:]
    odd[64:, 128:] = cas[:, :128]
    return even, odd


def split(value):
    high = value.astype(jnp.bfloat16)
    return high, (value - high.astype(jnp.float32)).astype(jnp.bfloat16)


def dot(left, right):
    return jnp.dot(left, right, preferred_element_type=jnp.float32)


def product(left, right):
    return dot(left[0], right[0]) + (dot(left[0], right[1]) + dot(left[1], right[0]))


def lane_transform(value, even_ref, odd_ref):
    even, odd = (even_ref[0], even_ref[1]), (odd_ref[0], odd_ref[1])
    high, low = split(value)
    tiles = []
    for start in range(0, LANES, 384):
        first = product((high[:, start : start + 256], low[:, start : start + 256]), even)
        last = product((high[:, start + 128 : start + 384], low[:, start + 128 : start + 384]), odd)
        tiles += [first[:, :128], first[:, 128:] + last[:, :128], last[:, 128:]]
    return jnp.concatenate(tiles, axis=1)


def forward_kernel(orbital_ref, band_ref, even_ref, odd_ref, rows_ref, out_ref):
    pair = orbital_ref[...] * band_ref[:, 0].reshape(N, LANES)
    spectrum = lane_transform(pair, even_ref, odd_ref)
    spectrum = product((rows_ref[0], rows_ref[1]), split(spectrum))
    for tile in range(TILES):
        out_ref[0, :, tile] = spectrum[:, 128 * tile : 128 * tile + 128].reshape(8, 24, 128)


def inverse_kernel(spectrum_ref, band_ref, sum_ref, even_ref, odd_ref, rows_ref, out_ref):
    member = pl.program_id(0)
    spectrum = jnp.concatenate(
        [spectrum_ref[0, :, tile].reshape(N, 128) for tile in range(TILES)], axis=1
    )
    potential = product((rows_ref[0], rows_ref[1]), split(spectrum))
    potential = lane_transform(potential, even_ref, odd_ref)
    prefactor = -1.0 / math.sqrt(N * 8)
    weight = jnp.where(member < 2, prefactor, 2.0 * prefactor)
    term = (weight * band_ref[:, 0].reshape(N, LANES)) * potential

    @pl.when(member == 0)
    def _():
        out_ref[...] = sum_ref[...] + term

    @pl.when(member > 0)
    def _():
        out_ref[...] += term


def filter_kernel(columns_ref, pair_ref, wave_ref, to_ref, from_ref, out_ref):
    source = columns_ref.reshape(32 * TILES * 8, 128)
    target = out_ref.reshape(32 * TILES * 8, 128)
    lower = lax.broadcasted_iota(jnp.int32, (32, 128), 1) < 64

    def rows(tile, k):
        return pl.ds(8 * tile + k, 32, stride=TILES * 8)

    blocks = []
    for k in range(8):
        tiles = [3 * (i // 2) + 2 * (i % 2) for i in range(6)]
        blocks.append(jnp.concatenate([source[rows(tile, k), :] for tile in tiles], axis=0))
    for k in range(0, 8, 2):
        parts = []
        for tile in (1, 4, 7):
            one, two = source[rows(tile, k), :], source[rows(tile, k + 1), :]
            parts.append(jnp.where(lower, one, pltpu.roll(two, 64, 1)))
            parts.append(jnp.where(lower, pltpu.roll(one, 64, 1), two))
        blocks.append(jnp.concatenate(parts, axis=0))
    columns = jnp.concatenate(blocks, axis=1)
    spectrum = product((to_ref[0], to_ref[1]), split(columns))
    spectrum = spectrum * ((4.0 * math.pi / float(N) ** 3) / (wave_ref[...] + pair_ref[0]))
    columns = product((from_ref[0], from_ref[1]), split(spectrum))
    for k in range(8):
        for i in range(6):
            tile = 3 * (i // 2) + 2 * (i % 2)
            target[rows(tile, k), :] = columns[32 * i : 32 * i + 32, 128 * k : 128 * k + 128]
    for k in range(0, 8, 2):
        start = 1024 + 64 * k
        for h in range(3):
            one = columns[64 * h : 64 * h + 32, start : start + 128]
            two = columns[64 * h + 32 : 64 * h + 64, start : start + 128]
            target[rows(3 * h + 1, k), :] = jnp.where(lower, one, pltpu.roll(two, 64, 1))
            target[rows(3 * h + 1, k + 1), :] = jnp.where(lower, pltpu.roll(one, 64, 1), two)


def whole(array):
    return pl.BlockSpec(array.shape, lambda step: (0,) * array.ndim)


PARAMS = pltpu.CompilerParams(vmem_limit_bytes=VMEM)
COST = pl.CostEstimate(flops=16 * 10**9, bytes_accessed=10**7, transcendentals=0)
BANDS = pl.BlockSpec((8, 1, 24, LANES), lambda step: (0, step, 0, 0))
SPECTRA = pl.BlockSpec((1, 8, TILES, 24, 128), lambda step: (step, 0, 0, 0, 0))
COLUMNS = pl.BlockSpec((32, TILES, 8, 128), lambda step: (0, 0, step, 0))


def forward(orbital, bands):
    even, odd = lane_matrices()
    even, odd = jnp.asarray(two_terms(even)), jnp.asarray(two_terms(odd))
    rows = jnp.asarray(two_terms(cas_matrix()[:, held_order()]))
    return pl.pallas_call(
        forward_kernel,
        grid=(4,),
        in_specs=[whole(orbital), BANDS, whole(even), whole(odd), whole(rows)],
        out_specs=SPECTRA,
        out_shape=jax.ShapeDtypeStruct((4, 8, TILES, 24, 128), jnp.float32),
        compiler_params=PARAMS,
        cost_estimate=COST,
        name="forward",
    )(orbital, bands, even, odd, rows)


def inverse(spectra, bands, total):
    even, odd = lane_matrices()
    even, odd = jnp.asarray(two_terms(even)), jnp.asarray(two_terms(odd.T))
    rows = jnp.asarray(two_terms(cas_matrix()[held_order(), :]))
    return pl.pallas_call(
        inverse_kernel,
        grid=(4,),
        in_specs=[SPECTRA, BANDS, whole(total), whole(even), whole(odd), whole(rows)],
        out_specs=whole(total),
        out_shape=jax.ShapeDtypeStruct((N, LANES), jnp.float32),
        compiler_params=PARAMS,
        cost_estimate=COST,
        name="inverse",
    )(spectra, bands, total, even, odd, rows)


def filtered(columns, pair_wave, wave):
    to = jnp.asarray(two_terms(cas_matrix()[:, column_order()]))
    back = jnp.asarray(two_terms(cas_matrix()[column_order(), :]))
    return pl.pallas_call(
        filter_kernel,
        grid=(3,),
        in_specs=[COLUMNS, pl.BlockSpec((1, 1, 8 * N), lambda step: (step, 0, 0)), whole(wave), whole(to), whole(back)],
        out_specs=COLUMNS,
        out_shape=jax.ShapeDtypeStruct((32, TILES, 24, 128), jnp.float32),
        compiler_params=PARAMS,
        cost_estimate=COST,
        name="filter",
    )(columns, pair_wave, wave, to, back)


def wavenumber(index):
    folded = jnp.minimum(index, N - index)
    return folded.astype(jnp.float32) * (2.0 * math.pi / N)


def filter_waves(place):
    wave = wavenumber(jnp.arange(N, dtype=jnp.int32)) ** 2
    mine = wavenumber((place % 8) * 24 + jnp.arange(24, dtype=jnp.int32)) ** 2
    screen = (4.0 * math.pi / N) ** 2
    pair = mine.reshape(3, 8, 1) + wave[None, None, :] + screen
    pair = jnp.concatenate([pair[:, :, :128].reshape(3, 1024), pair[:, :, 128:].reshape(3, 512)], axis=1)
    return pair.reshape(3, 1, 8 * N), wave.reshape(N, 1)


def exchange_plane(blocks):
    return lax.all_to_all(blocks, PLANE, 0, 0, tiled=True)


def exchange_z(blocks):
    return lax.all_to_all(blocks, "z", 0, 0, tiled=True)


def to_blocks(planes):
    count = planes.shape[0]
    blocks = planes.reshape(count, 6, 32, 6, N).transpose(2, 0, 1, 3, 4)
    return blocks.reshape(32, count * 54, 128)


def shards(resident, owned, owner):
    pair_wave, wave = filter_waves(lax.axis_index(PLANE))
    orbital = exchange_z(exchange_plane(to_blocks(resident)).reshape(8, 216, 128))
    orbital = orbital.reshape(N, LANES)
    halves = []
    for half in range(2):
        spread = exchange_plane(to_blocks(owned[0, 2 * half : 2 * half + 2])).reshape(8, 4, 108, 128)
        chosen = [lax.dynamic_index_in_dim(spread, owner[turn], 0, keepdims=False) for turn in range(2)]
        chosen = jnp.stack(chosen).reshape(2, 4, 2, 6, LANES).transpose(0, 2, 1, 3, 4)
        halves.append(lax.all_gather(chosen.reshape(4, 24, LANES), "z", axis=0, tiled=False))
    spectra = []
    for bands in halves:
        spectra.append(exchange_plane(forward(orbital, bands).reshape(32, TILES, 24, 128)))
    potentials = []
    for columns in spectra:
        potentials.append(exchange_plane(filtered(columns, pair_wave, wave)))
    total = jnp.zeros((N, LANES), jnp.float32)
    for bands, potential in zip(halves, potentials):
        total = inverse(potential.reshape(4, 8, TILES, 24, 128), bands, total)
    back = exchange_z(total.reshape(8, 216, 128))
    back = exchange_plane(back.reshape(32, 54, 128))
    return back.reshape(32, 6, 6, N).transpose(1, 0, 2, 3).reshape(1, 6, N, N)


def solution(mesh):
    fine = Mesh(mesh.devices.reshape(2, 4, 2, 8, 2), ("x_lo", "y", "x_hi", "z", "core"))
    band, slab = ("x_lo", "y"), ("x_hi", "z", "core")
    return jax.shard_map(
        shards,
        mesh=fine,
        in_specs=(P(band, slab), P(band, None, slab), P()),
        out_specs=P(band, slab),
        check_vma=False,
    )
```

```python
import functools
import math

import jax
import jax.numpy as jnp
import ml_dtypes
import numpy as np
from jax import lax
from jax.experimental import pallas as pl
from jax.experimental.pallas import tpu as pltpu
from jax.sharding import Mesh, PartitionSpec as P

N = 192
LANES = 6 * N
TILES = LANES // 128
PLANE = ("x_lo", "y", "x_hi", "core")
VMEM = 60 * 1024 * 1024


def cas_matrix():
    index = np.arange(N)
    phases = (index[:, None] * index[None, :] % N) * (2.0 * math.pi / N)
    return np.cos(phases) + np.sin(phases)


def held_order():
    z, x_hi, core, row = np.meshgrid(np.arange(8), np.arange(2), np.arange(2), np.arange(6), indexing="ij")
    return (6 * (x_hi * 16 + z * 2 + core) + row).reshape(-1)


def column_order():
    inner, device = np.meshgrid(np.arange(6), np.arange(32), indexing="ij")
    return (6 * device + inner).reshape(-1)


def two_terms(matrix):
    high = matrix.astype(np.float32).astype(ml_dtypes.bfloat16)
    low = (matrix - high.astype(np.float64)).astype(np.float32).astype(ml_dtypes.bfloat16)
    return np.stack([high, low])


def lane_matrices():
    cas = cas_matrix()
    even, odd = np.zeros((256, 256)), np.zeros((256, 256))
    even[:N, :N] = cas
    odd[64:, 64:128] = cas[:, 128:]
    odd[64:, 128:] = cas[:, :128]
    return even, odd


def split(value):
    high = value.astype(jnp.bfloat16)
    return high, (value - high.astype(jnp.float32)).astype(jnp.bfloat16)


def dot(left, right):
    return jnp.dot(left, right, preferred_element_type=jnp.float32)


def product(left, right):
    return dot(left[0], right[0]) + (dot(left[0], right[1]) + dot(left[1], right[0]))


def lane_transform(value, even_ref, odd_ref):
    even, odd = (even_ref[0], even_ref[1]), (odd_ref[0], odd_ref[1])
    high, low = split(value)
    tiles = []
    for start in range(0, LANES, 384):
        first = product((high[:, start : start + 256], low[:, start : start + 256]), even)
        last = product((high[:, start + 128 : start + 384], low[:, start + 128 : start + 384]), odd)
        tiles += [first[:, :128], first[:, 128:] + last[:, :128], last[:, 128:]]
    return jnp.concatenate(tiles, axis=1)


def pack_kernel(planes_ref, out_ref, left_ref, right_ref):
    fields, rows = planes_ref.shape[0], out_ref.shape[1]
    target = out_ref.reshape(32 * rows, 128)
    lower = lax.broadcasted_iota(jnp.int32, (32, 128), 1) < 64
    for field in range(fields):
        for a in range(6):
            slot = (6 * field + a) % 2
            left, right = left_ref.at[slot], right_ref.at[slot]
            left[...] = planes_ref[field, a, :, :128]
            right[:, :64] = planes_ref[field, a, :, 128:]
            for h in range(3):
                even, odd = pl.ds(2 * h, 32, stride=6), pl.ds(2 * h + 1, 32, stride=6)
                start = pltpu.roll(left[odd, :], 64, 1)
                end = pltpu.roll(right[odd, :], 64, 1)
                row = field * 54 + a * TILES + 3 * h
                target[pl.ds(row, 32, stride=rows), :] = left[even, :]
                target[pl.ds(row + 1, 32, stride=rows), :] = jnp.where(lower, right[even, :], start)
                target[pl.ds(row + 2, 32, stride=rows), :] = jnp.where(lower, start, end)


def slots_kernel(slots_ref, spread_ref, *out_refs):
    for slot, out_ref in enumerate(out_refs):
        for source in range(4):
            block = spread_ref.at[slots_ref[slot], source]
            for tile in range(TILES):
                rows = block[pl.ds(tile, 6, stride=TILES), :]
                out_ref[6 * source : 6 * source + 6, 128 * tile : 128 * tile + 128] = rows


def choose_kernel(owner_ref, spread_ref, out_ref):
    for source in range(4):
        block = spread_ref.at[0, source]
        for member in range(2):
            for tile in range(TILES):
                rows = block[pl.ds(54 * member + tile, 6, stride=TILES), :]
                out_ref[member, 6 * source : 6 * source + 6, 128 * tile : 128 * tile + 128] = rows


def forward_kernel(slots_ref, *refs):
    piece_refs, (band_ref, even_ref, odd_ref, rows_ref, out_ref, orbital_ref) = refs[:8], refs[8:]

    @pl.when(pl.program_id(0) == 0)
    def _():
        for slot, piece_ref in enumerate(piece_refs):
            orbital_ref[slots_ref[slot]] = piece_ref[...]

    pair = orbital_ref[...].reshape(N, LANES) * band_ref[:, 0].reshape(N, LANES)
    spectrum = lane_transform(pair, even_ref, odd_ref)
    spectrum = product((rows_ref[0], rows_ref[1]), split(spectrum))
    for tile in range(TILES):
        out_ref[0, :, tile] = spectrum[:, 128 * tile : 128 * tile + 128].reshape(8, 24, 128)


def inverse_kernel(spectrum_ref, band_ref, sum_ref, even_ref, odd_ref, rows_ref, out_ref):
    member = pl.program_id(0)
    spectrum = jnp.concatenate(
        [spectrum_ref[0, :, tile].reshape(N, 128) for tile in range(TILES)], axis=1
    )
    potential = product((rows_ref[0], rows_ref[1]), split(spectrum))
    potential = lane_transform(potential, even_ref, odd_ref)
    prefactor = -1.0 / math.sqrt(N * 8)
    weight = jnp.where(member < 2, prefactor, 2.0 * prefactor)
    term = (weight * band_ref[:, 0].reshape(N, LANES)) * potential

    @pl.when(member == 0)
    def _():
        out_ref[...] = sum_ref[...] + term

    @pl.when(member > 0)
    def _():
        out_ref[...] += term


def filter_kernel(columns_ref, pair_ref, wave_ref, to_ref, from_ref, out_ref):
    source = columns_ref.reshape(32 * TILES * 8, 128)
    target = out_ref.reshape(32 * TILES * 8, 128)
    lower = lax.broadcasted_iota(jnp.int32, (32, 128), 1) < 64

    def rows(tile, k):
        return pl.ds(8 * tile + k, 32, stride=TILES * 8)

    blocks = []
    for k in range(8):
        tiles = [3 * (i // 2) + 2 * (i % 2) for i in range(6)]
        blocks.append(jnp.concatenate([source[rows(tile, k), :] for tile in tiles], axis=0))
    for k in range(0, 8, 2):
        parts = []
        for tile in (1, 4, 7):
            one, two = source[rows(tile, k), :], source[rows(tile, k + 1), :]
            parts.append(jnp.where(lower, one, pltpu.roll(two, 64, 1)))
            parts.append(jnp.where(lower, pltpu.roll(one, 64, 1), two))
        blocks.append(jnp.concatenate(parts, axis=0))
    columns = jnp.concatenate(blocks, axis=1)
    spectrum = product((to_ref[0], to_ref[1]), split(columns))
    spectrum = spectrum * ((4.0 * math.pi / float(N) ** 3) / (wave_ref[...] + pair_ref[0]))
    columns = product((from_ref[0], from_ref[1]), split(spectrum))
    for k in range(8):
        for i in range(6):
            tile = 3 * (i // 2) + 2 * (i % 2)
            target[rows(tile, k), :] = columns[32 * i : 32 * i + 32, 128 * k : 128 * k + 128]
    for k in range(0, 8, 2):
        start = 1024 + 64 * k
        for h in range(3):
            one = columns[64 * h : 64 * h + 32, start : start + 128]
            two = columns[64 * h + 32 : 64 * h + 64, start : start + 128]
            target[rows(3 * h + 1, k), :] = jnp.where(lower, one, pltpu.roll(two, 64, 1))
            target[rows(3 * h + 1, k + 1), :] = jnp.where(lower, pltpu.roll(one, 64, 1), two)


def whole(array):
    return pl.BlockSpec(array.shape, lambda step: (0,) * array.ndim)


PARAMS = pltpu.CompilerParams(vmem_limit_bytes=VMEM)
COST = pl.CostEstimate(flops=16 * 10**9, bytes_accessed=10**7, transcendentals=0)
BANDS = pl.BlockSpec((8, 1, 24, LANES), lambda step: (0, step, 0, 0))
SPECTRA = pl.BlockSpec((1, 8, TILES, 24, 128), lambda step: (step, 0, 0, 0, 0))
COLUMNS = pl.BlockSpec((32, TILES, 8, 128), lambda step: (0, 0, step, 0))


MOVES = pltpu.CompilerParams(vmem_limit_bytes=16 * 1024 * 1024)
MOVED = pl.CostEstimate(flops=0, bytes_accessed=4 * 10**6, transcendentals=0)


def to_blocks(planes):
    rows = 56 * planes.shape[0]
    return pl.pallas_call(
        pack_kernel,
        out_shape=jax.ShapeDtypeStruct((32, rows, 128), jnp.float32),
        scratch_shapes=[pltpu.VMEM((2, N, 128), jnp.float32)] * 2,
        compiler_params=MOVES,
        cost_estimate=MOVED,
        name="pack",
    )(planes)


def by_slots(slots, spread):
    return pl.pallas_call(
        slots_kernel,
        in_specs=[pl.BlockSpec(memory_space=pltpu.SMEM), pl.BlockSpec(memory_space=pltpu.VMEM)],
        out_specs=[pl.BlockSpec(memory_space=pltpu.VMEM)] * 8,
        out_shape=[jax.ShapeDtypeStruct((24, LANES), jnp.float32)] * 8,
        compiler_params=MOVES,
        cost_estimate=MOVED,
        name="slots",
    )(slots, spread)


def choose(owner, spread):
    return pl.pallas_call(
        choose_kernel,
        grid_spec=pltpu.PrefetchScalarGridSpec(
            num_scalar_prefetch=1,
            grid=(2,),
            in_specs=[pl.BlockSpec((1, 4, 112, 128), lambda turn, owner: (owner[turn], 0, 0, 0))],
            out_specs=pl.BlockSpec((2, 24, LANES), lambda turn, owner: (turn, 0, 0)),
        ),
        out_shape=jax.ShapeDtypeStruct((4, 24, LANES), jnp.float32),
        compiler_params=MOVES,
        cost_estimate=MOVED,
        name="choose",
    )(owner, spread)


def forward(slots, pieces, bands):
    even, odd = lane_matrices()
    even, odd = jnp.asarray(two_terms(even)), jnp.asarray(two_terms(odd))
    rows = jnp.asarray(two_terms(cas_matrix()[:, held_order()]))
    return pl.pallas_call(
        forward_kernel,
        grid=(4,),
        in_specs=[
            pl.BlockSpec(memory_space=pltpu.SMEM),
            *[whole(piece) for piece in pieces],
            BANDS,
            whole(even),
            whole(odd),
            whole(rows),
        ],
        out_specs=SPECTRA,
        out_shape=jax.ShapeDtypeStruct((4, 8, TILES, 24, 128), jnp.float32),
        scratch_shapes=[pltpu.VMEM((8, 24, LANES), jnp.float32)],
        compiler_params=PARAMS,
        cost_estimate=COST,
        name="forward",
    )(slots, *pieces, bands, even, odd, rows)


def inverse(spectra, bands, total):
    even, odd = lane_matrices()
    even, odd = jnp.asarray(two_terms(even)), jnp.asarray(two_terms(odd.T))
    rows = jnp.asarray(two_terms(cas_matrix()[held_order(), :]))
    return pl.pallas_call(
        inverse_kernel,
        grid=(4,),
        in_specs=[SPECTRA, BANDS, whole(total), whole(even), whole(odd), whole(rows)],
        out_specs=whole(total),
        out_shape=jax.ShapeDtypeStruct((N, LANES), jnp.float32),
        compiler_params=PARAMS,
        cost_estimate=COST,
        name="inverse",
    )(spectra, bands, total, even, odd, rows)


def filtered(columns, pair_wave, wave):
    to = jnp.asarray(two_terms(cas_matrix()[:, column_order()]))
    back = jnp.asarray(two_terms(cas_matrix()[column_order(), :]))
    return pl.pallas_call(
        filter_kernel,
        grid=(3,),
        in_specs=[COLUMNS, pl.BlockSpec((1, 1, 8 * N), lambda step: (step, 0, 0)), whole(wave), whole(to), whole(back)],
        out_specs=COLUMNS,
        out_shape=jax.ShapeDtypeStruct((32, TILES, 24, 128), jnp.float32),
        compiler_params=PARAMS,
        cost_estimate=COST,
        name="filter",
    )(columns, pair_wave, wave, to, back)


def wavenumber(index):
    folded = jnp.minimum(index, N - index)
    return folded.astype(jnp.float32) * (2.0 * math.pi / N)


def filter_waves(place):
    wave = wavenumber(jnp.arange(N, dtype=jnp.int32)) ** 2
    mine = wavenumber((place % 8) * 24 + jnp.arange(24, dtype=jnp.int32)) ** 2
    screen = (4.0 * math.pi / N) ** 2
    pair = mine.reshape(3, 8, 1) + wave[None, None, :] + screen
    pair = jnp.concatenate([pair[:, :, :128].reshape(3, 1024), pair[:, :, 128:].reshape(3, 512)], axis=1)
    return pair.reshape(3, 1, 8 * N), wave.reshape(N, 1)


def exchange_plane(blocks):
    return lax.all_to_all(blocks, PLANE, 0, 0, tiled=True)


def exchange_z(blocks):
    return lax.all_to_all(blocks, "z", 0, 0, tiled=True)


def gather_orbital(spread, slots):
    pieces = by_slots(slots, spread)
    return [pieces[0]] + [
        lax.ppermute(pieces[m], "z", [(z, z ^ m) for z in range(8)]) for m in range(1, 8)
    ]


def shards(resident, owned, owner):
    pair_wave, wave = filter_waves(lax.axis_index(PLANE))
    slots = lax.axis_index("z") ^ jnp.arange(8, dtype=jnp.int32)
    spread = exchange_plane(to_blocks(resident))
    first, second = to_blocks(owned[0, :2]), to_blocks(owned[0, 2:])
    first, spread = lax.optimization_barrier((first, spread))
    orbital = gather_orbital(spread.reshape(8, 4, 56, 128), slots)
    first, orbital = lax.optimization_barrier((exchange_plane(first), orbital))
    first = choose(owner, first.reshape(8, 4, 112, 128))
    second, first = lax.optimization_barrier((second, first))
    halves = [lax.all_gather(first, "z", axis=0, tiled=False)]
    second = choose(owner, exchange_plane(second).reshape(8, 4, 112, 128))
    halves.append(lax.all_gather(second, "z", axis=0, tiled=False))
    spectra = []
    for bands in halves:
        spectra.append(exchange_plane(forward(slots, orbital, bands).reshape(32, 216, 128)))
    potentials = []
    for columns in spectra:
        columns = filtered(columns.reshape(32, TILES, 24, 128), pair_wave, wave)
        potentials.append(exchange_plane(columns.reshape(32, 216, 128)))
    total = jnp.zeros((N, LANES), jnp.float32)
    for bands, potential in zip(halves, potentials):
        total = inverse(potential.reshape(4, 8, TILES, 24, 128), bands, total)
    back = exchange_z(total.reshape(8, 216, 128))
    back = exchange_plane(back.reshape(32, 54, 128))
    return back.reshape(32, 6, 6, N).transpose(1, 0, 2, 3).reshape(1, 6, N, N)


def solution(mesh):
    fine = Mesh(mesh.devices.reshape(2, 4, 2, 8, 2), ("x_lo", "y", "x_hi", "z", "core"))
    band, slab = ("x_lo", "y"), ("x_hi", "z", "core")
    return jax.shard_map(
        shards,
        mesh=fine,
        in_specs=(P(band, slab), P(band, None, slab), P()),
        out_specs=P(band, slab),
        check_vma=False,
    )
```

```python
import functools
import math

import jax
import jax.numpy as jnp
import ml_dtypes
import numpy as np
from jax import lax
from jax.experimental import pallas as pl
from jax.experimental.pallas import tpu as pltpu
from jax.sharding import Mesh, PartitionSpec as P

N = 192
LANES = 6 * N
TILES = LANES // 128
PLANE = ("x_lo", "y", "x_hi", "core")
VMEM = 62 * 1024 * 1024


def cas_matrix():
    index = np.arange(N)
    phases = (index[:, None] * index[None, :] % N) * (2.0 * math.pi / N)
    return np.cos(phases) + np.sin(phases)


def held_order():
    z, x_hi, core, row = np.meshgrid(np.arange(8), np.arange(2), np.arange(2), np.arange(6), indexing="ij")
    return (6 * (x_hi * 16 + z * 2 + core) + row).reshape(-1)


def column_order():
    inner, device = np.meshgrid(np.arange(6), np.arange(32), indexing="ij")
    return (6 * device + inner).reshape(-1)


def two_terms(matrix):
    high = matrix.astype(np.float32).astype(ml_dtypes.bfloat16)
    low = (matrix - high.astype(np.float64)).astype(np.float32).astype(ml_dtypes.bfloat16)
    return np.stack([high, low])


def lane_matrices():
    cas = cas_matrix()
    even, odd = np.zeros((256, 256)), np.zeros((256, 256))
    even[:N, :N] = cas
    odd[64:, 64:128] = cas[:, 128:]
    odd[64:, 128:] = cas[:, :128]
    return even, odd


def split(value):
    high = value.astype(jnp.bfloat16)
    return high, (value - high.astype(jnp.float32)).astype(jnp.bfloat16)


def dot(left, right):
    return jnp.dot(left, right, preferred_element_type=jnp.float32)


def product(left, right):
    return dot(left[0], right[0]) + (dot(left[0], right[1]) + dot(left[1], right[0]))


def lane_transform(value, even_ref, odd_ref):
    even, odd = (even_ref[0], even_ref[1]), (odd_ref[0], odd_ref[1])
    high, low = split(value)
    tiles = []
    for start in range(0, LANES, 384):
        first = product((high[:, start : start + 256], low[:, start : start + 256]), even)
        last = product((high[:, start + 128 : start + 384], low[:, start + 128 : start + 384]), odd)
        tiles += [first[:, :128], first[:, 128:] + last[:, :128], last[:, 128:]]
    return jnp.concatenate(tiles, axis=1)


def pack_kernel(planes_ref, out_ref, left_ref, right_ref):
    fields, rows = planes_ref.shape[0], out_ref.shape[1]
    target = out_ref.reshape(32 * rows, 128)
    lower = lax.broadcasted_iota(jnp.int32, (32, 128), 1) < 64
    for field in range(fields):
        for a in range(6):
            slot = (6 * field + a) % 2
            left, right = left_ref.at[slot], right_ref.at[slot]
            left[...] = planes_ref[field, a, :, :128]
            right[:, :64] = planes_ref[field, a, :, 128:]
            for h in range(3):
                even, odd = pl.ds(2 * h, 32, stride=6), pl.ds(2 * h + 1, 32, stride=6)
                start = pltpu.roll(left[odd, :], 64, 1)
                end = pltpu.roll(right[odd, :], 64, 1)
                row = field * 54 + a * TILES + 3 * h
                target[pl.ds(row, 32, stride=rows), :] = left[even, :]
                target[pl.ds(row + 1, 32, stride=rows), :] = jnp.where(lower, right[even, :], start)
                target[pl.ds(row + 2, 32, stride=rows), :] = jnp.where(lower, start, end)


def slots_kernel(slots_ref, spread_ref, *out_refs):
    for slot, out_ref in enumerate(out_refs):
        for source in range(4):
            block = spread_ref.at[slots_ref[slot], source]
            for tile in range(TILES):
                rows = block[pl.ds(tile, 6, stride=TILES), :]
                out_ref[6 * source : 6 * source + 6, 128 * tile : 128 * tile + 128] = rows


def choose_kernel(owner_ref, spread_ref, out_ref):
    for source in range(4):
        block = spread_ref.at[0, source]
        for member in range(2):
            for tile in range(TILES):
                rows = block[pl.ds(54 * member + tile, 6, stride=TILES), :]
                out_ref[member, 6 * source : 6 * source + 6, 128 * tile : 128 * tile + 128] = rows


def forward_kernel(slots_ref, *refs):
    piece_refs, (band_ref, even_ref, odd_ref, rows_ref, out_ref, orbital_ref) = refs[:8], refs[8:]

    @pl.when(pl.program_id(0) == 0)
    def _():
        for slot, piece_ref in enumerate(piece_refs):
            orbital_ref[slots_ref[slot]] = piece_ref[...]

    pair = orbital_ref[...].reshape(N, LANES) * band_ref[:, 0].reshape(N, LANES)
    spectrum = lane_transform(pair, even_ref, odd_ref)
    spectrum = product((rows_ref[0], rows_ref[1]), split(spectrum))
    for tile in range(TILES):
        out_ref[0, :, tile] = spectrum[:, 128 * tile : 128 * tile + 128].reshape(8, 24, 128)


def inverse_kernel(spectrum_ref, first_ref, last_ref, even_ref, odd_ref, rows_ref, out_ref, total_ref):
    step = pl.program_id(0)
    spectrum = jnp.concatenate(
        [spectrum_ref[0, :, 0, tile].reshape(N, 128) for tile in range(TILES)], axis=1
    )
    potential = product((rows_ref[0], rows_ref[1]), split(spectrum))
    potential = lane_transform(potential, even_ref, odd_ref)
    prefactor = -1.0 / math.sqrt(N * 8)
    potential = jnp.where(step % 4 < 2, prefactor, 2.0 * prefactor) * potential

    @pl.when(step == 0)
    def _():
        total_ref[...] = first_ref[:, 0].reshape(N, LANES) * potential

    @pl.when((step > 0) & (step < 4))
    def _():
        total_ref[...] += first_ref[:, 0].reshape(N, LANES) * potential

    @pl.when(step >= 4)
    def _():
        total_ref[...] += last_ref[:, 0].reshape(N, LANES) * potential

    @pl.when(step == 7)
    def _():
        for z in range(8):
            for source in range(4):
                rows = pl.ds(24 * z + 6 * source, 6)
                for tile in range(TILES):
                    block = total_ref[rows, 128 * tile : 128 * tile + 128]
                    out_ref[z, 56 * source + 6 * tile : 56 * source + 6 * tile + 6, :] = block


def unpack_kernel(blocks_ref, out_ref, left_ref, right_ref):
    source = blocks_ref.reshape(32 * 56, 128)
    lower = lax.broadcasted_iota(jnp.int32, (32, 128), 1) < 64
    for a in range(6):
        left, right = left_ref.at[a % 2], right_ref.at[a % 2]
        for h in range(3):
            tiles = [source[pl.ds(18 * h + 6 * k + a, 32, stride=56), :] for k in range(3)]
            even, odd = pl.ds(2 * h, 32, stride=6), pl.ds(2 * h + 1, 32, stride=6)
            turned = pltpu.roll(tiles[2], 64, 1)
            left[even, :] = tiles[0]
            right[even, :] = tiles[1]
            left[odd, :] = jnp.where(lower, pltpu.roll(tiles[1], 64, 1), turned)
            right[odd, :] = turned
        out_ref[0, a, :, :128] = left[...]
        out_ref[0, a, :, 128:] = right[:, :64]


def filter_kernel(columns_ref, pair_ref, wave_ref, to_ref, from_ref, *refs):
    out_ref = refs[-1]
    source = columns_ref.reshape(32 * TILES * 8, 128)
    target = out_ref.reshape(32 * TILES * 8, 128)
    lower = lax.broadcasted_iota(jnp.int32, (32, 128), 1) < 64

    def rows(tile, k):
        return pl.ds(8 * tile + k, 32, stride=TILES * 8)

    blocks = []
    for k in range(8):
        tiles = [3 * (i // 2) + 2 * (i % 2) for i in range(6)]
        blocks.append(jnp.concatenate([source[rows(tile, k), :] for tile in tiles], axis=0))
    for k in range(0, 8, 2):
        parts = []
        for tile in (1, 4, 7):
            one, two = source[rows(tile, k), :], source[rows(tile, k + 1), :]
            parts.append(jnp.where(lower, one, pltpu.roll(two, 64, 1)))
            parts.append(jnp.where(lower, pltpu.roll(one, 64, 1), two))
        blocks.append(jnp.concatenate(parts, axis=0))
    columns = jnp.concatenate(blocks, axis=1)
    spectrum = product((to_ref[0], to_ref[1]), split(columns))
    spectrum = spectrum * ((4.0 * math.pi / float(N) ** 3) / (wave_ref[...] + pair_ref[0]))
    columns = product((from_ref[0], from_ref[1]), split(spectrum))
    for k in range(8):
        for i in range(6):
            tile = 3 * (i // 2) + 2 * (i % 2)
            target[rows(tile, k), :] = columns[32 * i : 32 * i + 32, 128 * k : 128 * k + 128]
    for k in range(0, 8, 2):
        start = 1024 + 64 * k
        for h in range(3):
            one = columns[64 * h : 64 * h + 32, start : start + 128]
            two = columns[64 * h + 32 : 64 * h + 64, start : start + 128]
            target[rows(3 * h + 1, k), :] = jnp.where(lower, one, pltpu.roll(two, 64, 1))
            target[rows(3 * h + 1, k + 1), :] = jnp.where(lower, pltpu.roll(one, 64, 1), two)


def whole(array):
    return pl.BlockSpec(array.shape, lambda step: (0,) * len(array.shape))


PARAMS = pltpu.CompilerParams(vmem_limit_bytes=VMEM)
COST = pl.CostEstimate(flops=16 * 10**9, bytes_accessed=10**7, transcendentals=0)
BANDS = pl.BlockSpec((8, 1, 24, LANES), lambda step: (0, step, 0, 0))
SPECTRA = pl.BlockSpec((1, 8, TILES, 24, 128), lambda step: (step, 0, 0, 0, 0))
COLUMNS = pl.BlockSpec((32, TILES, 8, 128), lambda step: (0, 0, step, 0))


MOVES = pltpu.CompilerParams(vmem_limit_bytes=16 * 1024 * 1024)
MOVED = pl.CostEstimate(flops=0, bytes_accessed=4 * 10**6, transcendentals=0)


def to_blocks(planes, count, part):
    return pl.pallas_call(
        pack_kernel,
        grid=(1,),
        in_specs=[pl.BlockSpec((count, 6, N, N), lambda step: (part, 0, 0, 0))],
        out_specs=pl.BlockSpec((32, 56 * count, 128), lambda step: (0, 0, 0)),
        out_shape=jax.ShapeDtypeStruct((32, 56 * count, 128), jnp.float32),
        scratch_shapes=[pltpu.VMEM((2, N, 128), jnp.float32)] * 2,
        compiler_params=PARAMS,
        cost_estimate=MOVED,
        name="pack",
    )(planes)


def from_blocks(blocks):
    return pl.pallas_call(
        unpack_kernel,
        out_shape=jax.ShapeDtypeStruct((1, 6, N, N), jnp.float32),
        scratch_shapes=[pltpu.VMEM((2, N, 128), jnp.float32)] * 2,
        compiler_params=MOVES,
        cost_estimate=MOVED,
        name="unpack",
    )(blocks)


def by_slots(slots, spread):
    return pl.pallas_call(
        slots_kernel,
        in_specs=[pl.BlockSpec(memory_space=pltpu.SMEM), pl.BlockSpec(memory_space=pltpu.VMEM)],
        out_specs=[pl.BlockSpec(memory_space=pltpu.VMEM)] * 8,
        out_shape=[jax.ShapeDtypeStruct((24, LANES), jnp.float32)] * 8,
        compiler_params=MOVES,
        cost_estimate=MOVED,
        name="slots",
    )(slots, spread)


def choose(owner, spread):
    return pl.pallas_call(
        choose_kernel,
        grid_spec=pltpu.PrefetchScalarGridSpec(
            num_scalar_prefetch=1,
            grid=(2,),
            in_specs=[pl.BlockSpec((1, 4, 112, 128), lambda turn, owner: (owner[turn], 0, 0, 0))],
            out_specs=pl.BlockSpec((2, 24, LANES), lambda turn, owner: (turn, 0, 0)),
        ),
        out_shape=jax.ShapeDtypeStruct((4, 24, LANES), jnp.float32),
        compiler_params=MOVES,
        cost_estimate=MOVED,
        name="choose",
    )(owner, spread)


def forward(slots, pieces, bands):
    even, odd = lane_matrices()
    even, odd = jnp.asarray(two_terms(even)), jnp.asarray(two_terms(odd))
    rows = jnp.asarray(two_terms(cas_matrix()[:, held_order()]))
    return pl.pallas_call(
        forward_kernel,
        grid=(4,),
        in_specs=[
            pl.BlockSpec(memory_space=pltpu.SMEM),
            *[whole(piece) for piece in pieces],
            BANDS,
            whole(even),
            whole(odd),
            whole(rows),
        ],
        out_specs=SPECTRA,
        out_shape=jax.ShapeDtypeStruct((4, 8, TILES, 24, 128), jnp.float32),
        scratch_shapes=[pltpu.VMEM((8, 24, LANES), jnp.float32)],
        compiler_params=PARAMS,
        cost_estimate=COST,
        name="forward",
    )(slots, *pieces, bands, even, odd, rows)


def inverse(spectra, bands):
    even, odd = lane_matrices()
    even, odd = jnp.asarray(two_terms(even)), jnp.asarray(two_terms(odd.T))
    rows = jnp.asarray(two_terms(cas_matrix()[held_order(), :]))
    out = jax.ShapeDtypeStruct((8, 224, 128), jnp.float32)
    return pl.pallas_call(
        inverse_kernel,
        grid=(8,),
        in_specs=[
            pl.BlockSpec((1, 8, 1, TILES, 24, 128), lambda step: (step % 4, 0, step // 4, 0, 0, 0)),
            pl.BlockSpec((8, 1, 24, LANES), lambda step: (0, jnp.minimum(step, 3), 0, 0)),
            pl.BlockSpec((8, 1, 24, LANES), lambda step: (0, jnp.maximum(step - 4, 0), 0, 0)),
            whole(even),
            whole(odd),
            whole(rows),
        ],
        out_specs=whole(out),
        out_shape=out,
        scratch_shapes=[pltpu.VMEM((N, LANES), jnp.float32)],
        compiler_params=PARAMS,
        cost_estimate=COST,
        name="inverse",
    )(spectra, *bands, even, odd, rows)


def filtered(columns, pair_wave, wave, half, *earlier):
    to = jnp.asarray(two_terms(cas_matrix()[:, column_order()]))
    back = jnp.asarray(two_terms(cas_matrix()[column_order(), :]))
    waves = pl.BlockSpec((1, 1, 8 * N), lambda step: (step, 0, 0))
    return pl.pallas_call(
        filter_kernel,
        grid=(3,),
        in_specs=[COLUMNS, waves, whole(wave), whole(to), whole(back), *[pl.BlockSpec(memory_space=pl.ANY) for _ in earlier]],
        out_specs=pl.BlockSpec((32, 1, TILES, 8, 128), lambda step: (0, half, 0, step, 0)),
        out_shape=jax.ShapeDtypeStruct((32, 2, TILES, 24, 128), jnp.float32),
        input_output_aliases={5: 0} if earlier else {},
        compiler_params=PARAMS,
        cost_estimate=COST,
        name="filter",
    )(columns, pair_wave, wave, to, back, *earlier)


def wavenumber(index):
    folded = jnp.minimum(index, N - index)
    return folded.astype(jnp.float32) * (2.0 * math.pi / N)


def filter_waves(place):
    wave = wavenumber(jnp.arange(N, dtype=jnp.int32)) ** 2
    mine = wavenumber((place % 8) * 24 + jnp.arange(24, dtype=jnp.int32)) ** 2
    screen = (4.0 * math.pi / N) ** 2
    pair = mine.reshape(3, 8, 1) + wave[None, None, :] + screen
    pair = jnp.concatenate([pair[:, :, :128].reshape(3, 1024), pair[:, :, 128:].reshape(3, 512)], axis=1)
    return pair.reshape(3, 1, 8 * N), wave.reshape(N, 1)


def exchange_plane(blocks):
    return lax.all_to_all(blocks, PLANE, 0, 0, tiled=True)


def exchange_z(blocks):
    return lax.all_to_all(blocks, "z", 0, 0, tiled=True)


def gather_orbital(spread, slots):
    pieces = by_slots(slots, spread)
    return [pieces[0]] + [
        lax.ppermute(pieces[m], "z", [(z, z ^ m) for z in range(8)]) for m in range(1, 8)
    ]


def shards(resident, owned, owner):
    pair_wave, wave = filter_waves(lax.axis_index(PLANE))
    slots = lax.axis_index("z") ^ jnp.arange(8, dtype=jnp.int32)
    first = exchange_plane(to_blocks(owned[0], 2, 0))
    spread, first = lax.optimization_barrier((to_blocks(resident, 1, 0), first))
    halves = [lax.all_gather(choose(owner, first.reshape(8, 4, 112, 128)), "z", axis=0, tiled=False)]
    spread = exchange_plane(spread)
    second, spread = lax.optimization_barrier((to_blocks(owned[0], 2, 1), spread))
    orbital = gather_orbital(spread.reshape(8, 4, 56, 128), slots)
    second, orbital = lax.optimization_barrier((exchange_plane(second), orbital))
    second = choose(owner, second.reshape(8, 4, 112, 128))
    halves.append(lax.all_gather(second, "z", axis=0, tiled=False))
    spectra = []
    for bands in halves:
        spectra.append(exchange_plane(forward(slots, orbital, bands).reshape(32, 216, 128)))
    columns = []
    for half, arrived in enumerate(spectra):
        columns = [filtered(arrived.reshape(32, TILES, 24, 128), pair_wave, wave, half, *columns)]
    potentials = exchange_plane(columns[0].reshape(32, 432, 128))
    total = inverse(potentials.reshape(4, 8, 2, TILES, 24, 128), halves)
    back = exchange_plane(exchange_z(total).reshape(32, 56, 128))
    return from_blocks(back)


def solution(mesh):
    fine = Mesh(mesh.devices.reshape(2, 4, 2, 8, 2), ("x_lo", "y", "x_hi", "z", "core"))
    band, slab = ("x_lo", "y"), ("x_hi", "z", "core")
    return jax.shard_map(
        shards,
        mesh=fine,
        in_specs=(P(band, slab), P(band, None, slab), P()),
        out_specs=P(band, slab),
        check_vma=False,
    )
```

```python
import functools
import math

import jax
import jax.numpy as jnp
import ml_dtypes
import numpy as np
from jax import lax
from jax.experimental import pallas as pl
from jax.experimental.pallas import tpu as pltpu
from jax.sharding import Mesh, PartitionSpec as P

N = 192
LANES = 6 * N
TILES = LANES // 128
PLANE = ("x_lo", "y", "x_hi", "core")
PARTS = 1
VMEM = 62 * 1024 * 1024


def cas_matrix():
    index = np.arange(N)
    phases = (index[:, None] * index[None, :] % N) * (2.0 * math.pi / N)
    return np.cos(phases) + np.sin(phases)


def held_order():
    z, x_hi, core, row = np.meshgrid(np.arange(8), np.arange(2), np.arange(2), np.arange(6), indexing="ij")
    return (6 * (x_hi * 16 + z * 2 + core) + row).reshape(-1)


def column_order():
    inner, device = np.meshgrid(np.arange(6), np.arange(32), indexing="ij")
    return (6 * device + inner).reshape(-1)


def two_terms(matrix):
    high = matrix.astype(np.float32).astype(ml_dtypes.bfloat16)
    low = (matrix - high.astype(np.float64)).astype(np.float32).astype(ml_dtypes.bfloat16)
    return np.stack([high, low])


def stacked_terms(matrix):
    high, low = two_terms(matrix)
    return jnp.asarray(np.concatenate([high, low, high], axis=1))


def lane_terms(matrix):
    high, low = two_terms(matrix)
    return jnp.asarray(np.concatenate([high, high, low], axis=0))


def lane_matrices():
    cas = cas_matrix()
    even, odd = np.zeros((256, 256)), np.zeros((256, 256))
    even[:N, :N] = cas
    odd[64:, 64:128] = cas[:, 128:]
    odd[64:, 128:] = cas[:, :128]
    return even, odd


def split(value):
    high = value.astype(jnp.bfloat16)
    return high, (value - high.astype(jnp.float32)).astype(jnp.bfloat16)


def dot(left, right):
    return jnp.dot(left, right, preferred_element_type=jnp.float32)


def left_product(matrix_ref, value):
    high, low = split(value)
    return dot(matrix_ref[...], jnp.concatenate([high, high, low], axis=0))


def right_product(high, low, matrix_ref):
    return dot(jnp.concatenate([high, low, high], axis=1), matrix_ref[...])


def lane_transform(value, even_ref, odd_ref):
    high, low = split(value)

    def stacked(terms, offset):
        return jnp.concatenate([terms[:, s + offset : s + offset + 256] for s in range(0, LANES, 384)], axis=0)

    first = right_product(stacked(high, 0), stacked(low, 0), even_ref)
    last = right_product(stacked(high, 128), stacked(low, 128), odd_ref)
    middle = first[:, 128:] + last[:, :128]
    tiles = []
    for start in range(0, 3 * N, N):
        for part in (first[:, :128], middle, last[:, 128:]):
            tiles.append(part[start : start + N])
    return jnp.concatenate(tiles, axis=1)


def pack_kernel(planes_ref, out_ref, left_ref, right_ref):
    fields, rows = planes_ref.shape[0], out_ref.shape[1]
    target = out_ref.reshape(32 * rows, 128)
    lower = lax.broadcasted_iota(jnp.int32, (32, 128), 1) < 64
    for field in range(fields):
        for a in range(6):
            slot = (6 * field + a) % 2
            left, right = left_ref.at[slot], right_ref.at[slot]
            left[...] = planes_ref[field, a, :, :128]
            right[:, :64] = planes_ref[field, a, :, 128:]
            for h in range(3):
                even, odd = pl.ds(2 * h, 32, stride=6), pl.ds(2 * h + 1, 32, stride=6)
                start = pltpu.roll(left[odd, :], 64, 1)
                end = pltpu.roll(right[odd, :], 64, 1)
                row = field * 54 + a * TILES + 3 * h
                target[pl.ds(row, 32, stride=rows), :] = left[even, :]
                target[pl.ds(row + 1, 32, stride=rows), :] = jnp.where(lower, right[even, :], start)
                target[pl.ds(row + 2, 32, stride=rows), :] = jnp.where(lower, start, end)


def slots_kernel(slots_ref, spread_ref, *out_refs):
    for slot, out_ref in enumerate(out_refs):
        for source in range(4):
            block = spread_ref.at[slots_ref[slot], source]
            for tile in range(TILES):
                rows = block[pl.ds(tile, 6, stride=TILES), :]
                out_ref[6 * source : 6 * source + 6, 128 * tile : 128 * tile + 128] = rows


def choose_kernel(owner_ref, spread_ref, out_ref):
    for source in range(4):
        block = spread_ref.at[0, source]
        for member in range(2):
            for tile in range(TILES):
                rows = block[pl.ds(54 * member + tile, 6, stride=TILES), :]
                out_ref[member, 6 * source : 6 * source + 6, 128 * tile : 128 * tile + 128] = rows


def forward_kernel(slots_ref, *refs):
    piece_refs, (band_ref, even_ref, odd_ref, rows_ref, out_ref, orbital_ref) = refs[:8], refs[8:]

    @pl.when(pl.program_id(0) == 0)
    def _():
        for slot, piece_ref in enumerate(piece_refs):
            orbital_ref[slots_ref[slot]] = piece_ref[...]

    pair = orbital_ref[...].reshape(N, LANES) * band_ref[:, 0].reshape(N, LANES)
    spectrum = lane_transform(pair, even_ref, odd_ref)
    spectrum = left_product(rows_ref, spectrum)
    for tile in range(TILES):
        out_ref[0, :, tile] = spectrum[:, 128 * tile : 128 * tile + 128].reshape(8, 24, 128)


def joined(refs):
    return jnp.concatenate([ref[:, 0].reshape(N // PARTS, LANES) for ref in refs], axis=0)


def inverse_kernel(*refs):
    spectrum_refs, first_refs, last_refs = refs[:PARTS], refs[PARTS : 2 * PARTS], refs[2 * PARTS : 3 * PARTS]
    even_ref, odd_ref, rows_ref, out_ref, total_ref = refs[3 * PARTS :]
    step = pl.program_id(0)
    spectrum = []
    for ref in spectrum_refs:
        tiles = [ref[0, :, 0, tile].reshape(N // PARTS, 128) for tile in range(TILES)]
        spectrum.append(jnp.concatenate(tiles, axis=1))
    spectrum = jnp.concatenate(spectrum, axis=0)
    potential = left_product(rows_ref, spectrum)
    potential = lane_transform(potential, even_ref, odd_ref)
    prefactor = -1.0 / math.sqrt(N * 8)
    potential = jnp.where(step % 4 < 2, prefactor, 2.0 * prefactor) * potential

    @pl.when(step == 0)
    def _():
        total_ref[...] = joined(first_refs) * potential

    @pl.when((step > 0) & (step < 4))
    def _():
        total_ref[...] += joined(first_refs) * potential

    @pl.when(step >= 4)
    def _():
        total_ref[...] += joined(last_refs) * potential

    @pl.when(step == 7)
    def _():
        for z in range(8):
            for source in range(4):
                rows = pl.ds(24 * z + 6 * source, 6)
                for tile in range(TILES):
                    block = total_ref[rows, 128 * tile : 128 * tile + 128]
                    out_ref[z, 56 * source + 6 * tile : 56 * source + 6 * tile + 6, :] = block


def unpack_kernel(blocks_ref, out_ref, left_ref, right_ref):
    source = blocks_ref.reshape(32 * 56, 128)
    lower = lax.broadcasted_iota(jnp.int32, (32, 128), 1) < 64
    for a in range(6):
        left, right = left_ref.at[a % 2], right_ref.at[a % 2]
        for h in range(3):
            tiles = [source[pl.ds(18 * h + 6 * k + a, 32, stride=56), :] for k in range(3)]
            even, odd = pl.ds(2 * h, 32, stride=6), pl.ds(2 * h + 1, 32, stride=6)
            turned = pltpu.roll(tiles[2], 64, 1)
            left[even, :] = tiles[0]
            right[even, :] = tiles[1]
            left[odd, :] = jnp.where(lower, pltpu.roll(tiles[1], 64, 1), turned)
            right[odd, :] = turned
        out_ref[0, a, :, :128] = left[...]
        out_ref[0, a, :, 128:] = right[:, :64]


def filter_kernel(columns_ref, pair_ref, wave_ref, to_ref, from_ref, *refs):
    out_ref = refs[-1]
    source = columns_ref.reshape(32 * TILES * 8, 128)
    target = out_ref.reshape(32 * TILES * 8, 128)
    lower = lax.broadcasted_iota(jnp.int32, (32, 128), 1) < 64

    def rows(tile, k):
        return pl.ds(8 * tile + k, 32, stride=TILES * 8)

    blocks = []
    for k in range(8):
        tiles = [3 * (i // 2) + 2 * (i % 2) for i in range(6)]
        blocks.append(jnp.concatenate([source[rows(tile, k), :] for tile in tiles], axis=0))
    for k in range(0, 8, 2):
        parts = []
        for tile in (1, 4, 7):
            one, two = source[rows(tile, k), :], source[rows(tile, k + 1), :]
            parts.append(jnp.where(lower, one, pltpu.roll(two, 64, 1)))
            parts.append(jnp.where(lower, pltpu.roll(one, 64, 1), two))
        blocks.append(jnp.concatenate(parts, axis=0))
    columns = jnp.concatenate(blocks, axis=1)
    spectrum = left_product(to_ref, columns)
    spectrum = spectrum * ((4.0 * math.pi / float(N) ** 3) / (wave_ref[...] + pair_ref[0]))
    columns = left_product(from_ref, spectrum)
    for k in range(8):
        for i in range(6):
            tile = 3 * (i // 2) + 2 * (i % 2)
            target[rows(tile, k), :] = columns[32 * i : 32 * i + 32, 128 * k : 128 * k + 128]
    for k in range(0, 8, 2):
        start = 1024 + 64 * k
        for h in range(3):
            one = columns[64 * h : 64 * h + 32, start : start + 128]
            two = columns[64 * h + 32 : 64 * h + 64, start : start + 128]
            target[rows(3 * h + 1, k), :] = jnp.where(lower, one, pltpu.roll(two, 64, 1))
            target[rows(3 * h + 1, k + 1), :] = jnp.where(lower, pltpu.roll(one, 64, 1), two)


def whole(array):
    return pl.BlockSpec(array.shape, lambda step: (0,) * len(array.shape))


PARAMS = pltpu.CompilerParams(vmem_limit_bytes=VMEM)
COST = pl.CostEstimate(flops=16 * 10**9, bytes_accessed=10**7, transcendentals=0)
BANDS = pl.BlockSpec((8, 1, 24, LANES), lambda step: (0, step, 0, 0))
SPECTRA = pl.BlockSpec((1, 8, TILES, 24, 128), lambda step: (step, 0, 0, 0, 0))
COLUMNS = pl.BlockSpec((32, TILES, 8, 128), lambda step: (0, 0, step, 0))


MOVES = pltpu.CompilerParams(vmem_limit_bytes=16 * 1024 * 1024)
MOVED = pl.CostEstimate(flops=0, bytes_accessed=4 * 10**6, transcendentals=0)


def to_blocks(planes, count, part):
    return pl.pallas_call(
        pack_kernel,
        grid=(1,),
        in_specs=[pl.BlockSpec((count, 6, N, N), lambda step: (part, 0, 0, 0))],
        out_specs=pl.BlockSpec((32, 56 * count, 128), lambda step: (0, 0, 0)),
        out_shape=jax.ShapeDtypeStruct((32, 56 * count, 128), jnp.float32),
        scratch_shapes=[pltpu.VMEM((2, N, 128), jnp.float32)] * 2,
        compiler_params=PARAMS,
        cost_estimate=MOVED,
        name="pack",
    )(planes)


def in_parts(shape, dim, place):
    block = shape[:dim] + (shape[dim] // PARTS,) + shape[dim + 1 :]

    def part_place(part, step):
        at = place(step)
        return at[:dim] + (part,) + at[dim + 1 :]

    return [pl.BlockSpec(block, functools.partial(part_place, part)) for part in range(PARTS)]


def from_blocks(blocks):
    return pl.pallas_call(
        unpack_kernel,
        out_shape=jax.ShapeDtypeStruct((1, 6, N, N), jnp.float32),
        scratch_shapes=[pltpu.VMEM((2, N, 128), jnp.float32)] * 2,
        compiler_params=MOVES,
        cost_estimate=MOVED,
        name="unpack",
    )(blocks)


def by_slots(slots, spread):
    return pl.pallas_call(
        slots_kernel,
        in_specs=[pl.BlockSpec(memory_space=pltpu.SMEM), pl.BlockSpec(memory_space=pltpu.VMEM)],
        out_specs=[pl.BlockSpec(memory_space=pltpu.VMEM)] * 8,
        out_shape=[jax.ShapeDtypeStruct((24, LANES), jnp.float32)] * 8,
        compiler_params=MOVES,
        cost_estimate=MOVED,
        name="slots",
    )(slots, spread)


def choose(owner, spread):
    return pl.pallas_call(
        choose_kernel,
        grid_spec=pltpu.PrefetchScalarGridSpec(
            num_scalar_prefetch=1,
            grid=(2,),
            in_specs=[pl.BlockSpec((1, 4, 112, 128), lambda turn, owner: (owner[turn], 0, 0, 0))],
            out_specs=pl.BlockSpec((2, 24, LANES), lambda turn, owner: (turn, 0, 0)),
        ),
        out_shape=jax.ShapeDtypeStruct((4, 24, LANES), jnp.float32),
        compiler_params=MOVES,
        cost_estimate=MOVED,
        name="choose",
    )(owner, spread)


def forward(slots, pieces, bands):
    even, odd = lane_matrices()
    even, odd = lane_terms(even), lane_terms(odd)
    rows = stacked_terms(cas_matrix()[:, held_order()])
    return pl.pallas_call(
        forward_kernel,
        grid=(4,),
        in_specs=[
            pl.BlockSpec(memory_space=pltpu.SMEM),
            *[whole(piece) for piece in pieces],
            BANDS,
            whole(even),
            whole(odd),
            whole(rows),
        ],
        out_specs=SPECTRA,
        out_shape=jax.ShapeDtypeStruct((4, 8, TILES, 24, 128), jnp.float32),
        scratch_shapes=[pltpu.VMEM((8, 24, LANES), jnp.float32)],
        compiler_params=PARAMS,
        cost_estimate=COST,
        name="forward",
    )(slots, *pieces, bands, even, odd, rows)


def inverse(spectra, bands):
    even, odd = lane_matrices()
    even, odd = lane_terms(even), lane_terms(odd.T)
    rows = stacked_terms(cas_matrix()[held_order(), :])
    out = jax.ShapeDtypeStruct((8, 224, 128), jnp.float32)
    return pl.pallas_call(
        inverse_kernel,
        grid=(8,),
        in_specs=[
            *in_parts((1, 8, 1, TILES, 24, 128), 1, lambda step: (step % 4, 0, step // 4, 0, 0, 0)),
            *in_parts((8, 1, 24, LANES), 0, lambda step: (0, jnp.minimum(step, 3), 0, 0)),
            *in_parts((8, 1, 24, LANES), 0, lambda step: (0, jnp.maximum(step - 4, 0), 0, 0)),
            whole(even),
            whole(odd),
            whole(rows),
        ],
        out_specs=whole(out),
        out_shape=out,
        scratch_shapes=[pltpu.VMEM((N, LANES), jnp.float32)],
        compiler_params=pltpu.CompilerParams(vmem_limit_bytes=32 * 1024 * 1024),
        cost_estimate=COST,
        name="inverse",
    )(*[spectra] * PARTS, *[bands[0]] * PARTS, *[bands[1]] * PARTS, even, odd, rows)


def filtered(columns, pair_wave, wave, half, *earlier):
    to = stacked_terms(cas_matrix()[:, column_order()])
    back = stacked_terms(cas_matrix()[column_order(), :])
    waves = pl.BlockSpec((1, 1, 8 * N), lambda step: (step, 0, 0))
    return pl.pallas_call(
        filter_kernel,
        grid=(3,),
        in_specs=[COLUMNS, waves, whole(wave), whole(to), whole(back), *[pl.BlockSpec(memory_space=pl.ANY) for _ in earlier]],
        out_specs=pl.BlockSpec((32, 1, TILES, 8, 128), lambda step: (0, half, 0, step, 0)),
        out_shape=jax.ShapeDtypeStruct((32, 2, TILES, 24, 128), jnp.float32),
        input_output_aliases={5: 0} if earlier else {},
        compiler_params=PARAMS,
        cost_estimate=COST,
        name="filter",
    )(columns, pair_wave, wave, to, back, *earlier)


def wavenumber(index):
    folded = jnp.minimum(index, N - index)
    return folded.astype(jnp.float32) * (2.0 * math.pi / N)


def filter_waves(place):
    wave = wavenumber(jnp.arange(N, dtype=jnp.int32)) ** 2
    mine = wavenumber((place % 8) * 24 + jnp.arange(24, dtype=jnp.int32)) ** 2
    screen = (4.0 * math.pi / N) ** 2
    pair = mine.reshape(3, 8, 1) + wave[None, None, :] + screen
    pair = jnp.concatenate([pair[:, :, :128].reshape(3, 1024), pair[:, :, 128:].reshape(3, 512)], axis=1)
    return pair.reshape(3, 1, 8 * N), wave.reshape(N, 1)


def exchange_plane(blocks):
    return lax.all_to_all(blocks, PLANE, 0, 0, tiled=True)


def exchange_z(blocks):
    return lax.all_to_all(blocks, "z", 0, 0, tiled=True)


SHIFTS = (0, 4, 3, 5, 2, 6, 1, 7)


def gather_orbital(spread, place):
    shifts = jnp.array(SHIFTS, jnp.int32)
    pieces = by_slots((place + shifts) % 8, spread)
    moved = [
        lax.ppermute(piece, "z", [(z, (z + shift) % 8) for z in range(8)])
        for piece, shift in zip(pieces[1:], SHIFTS[1:])
    ]
    return [pieces[0]] + moved, (place - shifts) % 8


def shards(resident, owned, owner):
    pair_wave, wave = filter_waves(lax.axis_index(PLANE))
    first = exchange_plane(to_blocks(owned[0], 2, 0))
    spread, first = lax.optimization_barrier((to_blocks(resident, 1, 0), first))
    halves = [lax.all_gather(choose(owner, first.reshape(8, 4, 112, 128)), "z", axis=0, tiled=False)]
    spread = exchange_plane(spread)
    second, spread = lax.optimization_barrier((to_blocks(owned[0], 2, 1), spread))
    orbital, slots = gather_orbital(spread.reshape(8, 4, 56, 128), lax.axis_index("z"))
    second, orbital = lax.optimization_barrier((exchange_plane(second), orbital))
    second = choose(owner, second.reshape(8, 4, 112, 128))
    halves.append(lax.all_gather(second, "z", axis=0, tiled=False))
    spectra = []
    for bands in halves:
        spectra.append(exchange_plane(forward(slots, orbital, bands).reshape(32, 216, 128)))
    columns = []
    for half, arrived in enumerate(spectra):
        columns = [filtered(arrived.reshape(32, TILES, 24, 128), pair_wave, wave, half, *columns)]
    potentials = exchange_plane(columns[0].reshape(32, 432, 128))
    total = inverse(potentials.reshape(4, 8, 2, TILES, 24, 128), halves)
    back = exchange_plane(exchange_z(total).reshape(32, 56, 128))
    return from_blocks(back)


def solution(mesh):
    fine = Mesh(mesh.devices.reshape(2, 4, 2, 8, 2), ("x_lo", "y", "x_hi", "z", "core"))
    band, slab = ("x_lo", "y"), ("x_hi", "z", "core")
    return jax.shard_map(
        shards,
        mesh=fine,
        in_specs=(P(band, slab), P(band, None, slab), P()),
        out_specs=P(band, slab),
        check_vma=False,
    )
```

```python
import functools
import math

import jax
import jax.numpy as jnp
import ml_dtypes
import numpy as np
from jax import lax
from jax.experimental import pallas as pl
from jax.experimental.pallas import tpu as pltpu
from jax.sharding import Mesh, PartitionSpec as P

N = 192
LANES = 6 * N
TILES = LANES // 128
PLANE = ("x_lo", "y", "x_hi", "core")
PARTS = 1
VMEM = 62 * 1024 * 1024


def cas_matrix():
    index = np.arange(N)
    phases = (index[:, None] * index[None, :] % N) * (2.0 * math.pi / N)
    return np.cos(phases) + np.sin(phases)


def held_order():
    z, x_hi, core, row = np.meshgrid(np.arange(8), np.arange(2), np.arange(2), np.arange(6), indexing="ij")
    return (6 * (x_hi * 16 + z * 2 + core) + row).reshape(-1)


def column_order():
    inner, device = np.meshgrid(np.arange(6), np.arange(32), indexing="ij")
    return (6 * device + inner).reshape(-1)


def two_terms(matrix):
    high = matrix.astype(np.float32).astype(ml_dtypes.bfloat16)
    low = (matrix - high.astype(np.float64)).astype(np.float32).astype(ml_dtypes.bfloat16)
    return np.stack([high, low])


def stacked_terms(matrix):
    high, low = two_terms(matrix)
    return jnp.asarray(np.concatenate([high, low, high], axis=1))


def lane_terms(matrix):
    high, low = two_terms(matrix)
    return jnp.asarray(np.concatenate([high, high, low], axis=0))


def lane_matrices():
    cas = cas_matrix()
    even, odd = np.zeros((256, 256)), np.zeros((256, 256))
    even[:N, :N] = cas
    odd[64:, 64:128] = cas[:, 128:]
    odd[64:, 128:] = cas[:, :128]
    return even, odd


def split(value):
    high = value.astype(jnp.bfloat16)
    return high, (value - high.astype(jnp.float32)).astype(jnp.bfloat16)


def dot(left, right):
    return jnp.dot(left, right, preferred_element_type=jnp.float32)


def left_product(matrix_ref, value):
    high, low = split(value)
    return dot(matrix_ref[...], jnp.concatenate([high, high, low], axis=0))


def right_product(high, low, matrix_ref):
    return dot(jnp.concatenate([high, low, high], axis=1), matrix_ref[...])


def lane_transform(value, even_ref, odd_ref):
    high, low = split(value)

    def stacked(terms, offset):
        return jnp.concatenate([terms[:, s + offset : s + offset + 256] for s in range(0, LANES, 384)], axis=0)

    first = right_product(stacked(high, 0), stacked(low, 0), even_ref)
    last = right_product(stacked(high, 128), stacked(low, 128), odd_ref)
    middle = first[:, 128:] + last[:, :128]
    tiles = []
    for start in range(0, 3 * N, N):
        for part in (first[:, :128], middle, last[:, 128:]):
            tiles.append(part[start : start + N])
    return jnp.concatenate(tiles, axis=1)


def pack_kernel(planes_ref, out_ref, left_ref, right_ref):
    fields, rows = planes_ref.shape[0], out_ref.shape[1]
    target = out_ref.reshape(32 * rows, 128)
    lower = lax.broadcasted_iota(jnp.int32, (32, 128), 1) < 64
    for field in range(fields):
        for a in range(6):
            slot = (6 * field + a) % 2
            left, right = left_ref.at[slot], right_ref.at[slot]
            left[...] = planes_ref[field, a, :, :128]
            right[:, :64] = planes_ref[field, a, :, 128:]
            for h in range(3):
                even, odd = pl.ds(2 * h, 32, stride=6), pl.ds(2 * h + 1, 32, stride=6)
                start = pltpu.roll(left[odd, :], 64, 1)
                end = pltpu.roll(right[odd, :], 64, 1)
                row = field * 54 + a * TILES + 3 * h
                target[pl.ds(row, 32, stride=rows), :] = left[even, :]
                target[pl.ds(row + 1, 32, stride=rows), :] = jnp.where(lower, right[even, :], start)
                target[pl.ds(row + 2, 32, stride=rows), :] = jnp.where(lower, start, end)


def slots_kernel(slots_ref, spread_ref, *out_refs):
    for slot, out_ref in enumerate(out_refs):
        for source in range(4):
            block = spread_ref.at[slots_ref[slot], source]
            for tile in range(TILES):
                rows = block[pl.ds(tile, 6, stride=TILES), :]
                out_ref[6 * source : 6 * source + 6, 128 * tile : 128 * tile + 128] = rows


def choose_kernel(owner_ref, spread_ref, out_ref):
    for source in range(4):
        block = spread_ref.at[0, source]
        for member in range(2):
            for tile in range(TILES):
                rows = block[pl.ds(54 * member + tile, 6, stride=TILES), :]
                out_ref[member, 6 * source : 6 * source + 6, 128 * tile : 128 * tile + 128] = rows


def forward_kernel(slots_ref, *refs):
    piece_refs, (band_ref, even_ref, odd_ref, rows_ref, out_ref, orbital_ref) = refs[:8], refs[8:]

    @pl.when(pl.program_id(0) == 0)
    def _():
        for slot, piece_ref in enumerate(piece_refs):
            orbital_ref[slots_ref[slot]] = piece_ref[...]

    pair = orbital_ref[...].reshape(N, LANES) * band_ref[:, 0].reshape(N, LANES)
    spectrum = lane_transform(pair, even_ref, odd_ref)
    spectrum = left_product(rows_ref, spectrum)
    for tile in range(TILES):
        out_ref[0, :, tile] = spectrum[:, 128 * tile : 128 * tile + 128].reshape(8, 24, 128)


def joined(refs):
    return jnp.concatenate([ref[:, 0].reshape(N // PARTS, LANES) for ref in refs], axis=0)


def inverse_kernel(*refs):
    spectrum_refs, first_refs, last_refs = refs[:PARTS], refs[PARTS : 2 * PARTS], refs[2 * PARTS : 3 * PARTS]
    even_ref, odd_ref, rows_ref, out_ref, total_ref = refs[3 * PARTS :]
    step = pl.program_id(0)
    spectrum = []
    for ref in spectrum_refs:
        tiles = [ref[0, :, 0, tile].reshape(N // PARTS, 128) for tile in range(TILES)]
        spectrum.append(jnp.concatenate(tiles, axis=1))
    spectrum = jnp.concatenate(spectrum, axis=0)
    potential = left_product(rows_ref, spectrum)
    potential = lane_transform(potential, even_ref, odd_ref)
    prefactor = -1.0 / math.sqrt(N * 8)
    potential = jnp.where(step % 4 < 2, prefactor, 2.0 * prefactor) * potential

    @pl.when(step == 0)
    def _():
        total_ref[...] = joined(first_refs) * potential

    @pl.when((step > 0) & (step < 4))
    def _():
        total_ref[...] += joined(first_refs) * potential

    @pl.when(step >= 4)
    def _():
        total_ref[...] += joined(last_refs) * potential

    @pl.when(step == 7)
    def _():
        for z in range(8):
            for source in range(4):
                rows = pl.ds(24 * z + 6 * source, 6)
                for tile in range(TILES):
                    block = total_ref[rows, 128 * tile : 128 * tile + 128]
                    out_ref[z, 56 * source + 6 * tile : 56 * source + 6 * tile + 6, :] = block


def unpack_kernel(blocks_ref, out_ref, left_ref, right_ref):
    source = blocks_ref.reshape(32 * 56, 128)
    lower = lax.broadcasted_iota(jnp.int32, (32, 128), 1) < 64
    for a in range(6):
        left, right = left_ref.at[a % 2], right_ref.at[a % 2]
        for h in range(3):
            tiles = [source[pl.ds(18 * h + 6 * k + a, 32, stride=56), :] for k in range(3)]
            even, odd = pl.ds(2 * h, 32, stride=6), pl.ds(2 * h + 1, 32, stride=6)
            turned = pltpu.roll(tiles[2], 64, 1)
            left[even, :] = tiles[0]
            right[even, :] = tiles[1]
            left[odd, :] = jnp.where(lower, pltpu.roll(tiles[1], 64, 1), turned)
            right[odd, :] = turned
        out_ref[0, a, :, :128] = left[...]
        out_ref[0, a, :, 128:] = right[:, :64]


def filter_block(columns_ref, pair_ref, wave_ref, to_ref, from_ref, out_ref):
    source = columns_ref.reshape(32 * TILES * 8, 128)
    target = out_ref.reshape(32 * TILES * 8, 128)
    lower = lax.broadcasted_iota(jnp.int32, (32, 128), 1) < 64

    def rows(tile, k):
        return pl.ds(8 * tile + k, 32, stride=TILES * 8)

    blocks = []
    for k in range(8):
        tiles = [3 * (i // 2) + 2 * (i % 2) for i in range(6)]
        blocks.append(jnp.concatenate([source[rows(tile, k), :] for tile in tiles], axis=0))
    for k in range(0, 8, 2):
        parts = []
        for tile in (1, 4, 7):
            one, two = source[rows(tile, k), :], source[rows(tile, k + 1), :]
            parts.append(jnp.where(lower, one, pltpu.roll(two, 64, 1)))
            parts.append(jnp.where(lower, pltpu.roll(one, 64, 1), two))
        blocks.append(jnp.concatenate(parts, axis=0))
    columns = jnp.concatenate(blocks, axis=1)
    spectrum = left_product(to_ref, columns)
    spectrum = spectrum * ((4.0 * math.pi / float(N) ** 3) / (wave_ref[...] + pair_ref[0]))
    columns = left_product(from_ref, spectrum)
    for k in range(8):
        for i in range(6):
            tile = 3 * (i // 2) + 2 * (i % 2)
            target[rows(tile, k), :] = columns[32 * i : 32 * i + 32, 128 * k : 128 * k + 128]
    for k in range(0, 8, 2):
        start = 1024 + 64 * k
        for h in range(3):
            one = columns[64 * h : 64 * h + 32, start : start + 128]
            two = columns[64 * h + 32 : 64 * h + 64, start : start + 128]
            target[rows(3 * h + 1, k), :] = jnp.where(lower, one, pltpu.roll(two, 64, 1))
            target[rows(3 * h + 1, k + 1), :] = jnp.where(lower, pltpu.roll(one, 64, 1), two)


def filter_kernel(first_ref, last_ref, *refs):
    step = pl.program_id(0)

    @pl.when(step < 3)
    def _():
        filter_block(first_ref, *refs)

    @pl.when(step >= 3)
    def _():
        filter_block(last_ref, *refs)


def whole(array):
    return pl.BlockSpec(array.shape, lambda step: (0,) * len(array.shape))


PARAMS = pltpu.CompilerParams(vmem_limit_bytes=VMEM)
COST = pl.CostEstimate(flops=16 * 10**9, bytes_accessed=10**7, transcendentals=0)
BANDS = pl.BlockSpec((8, 1, 24, LANES), lambda step: (0, step, 0, 0))
SPECTRA = pl.BlockSpec((1, 8, TILES, 24, 128), lambda step: (step, 0, 0, 0, 0))


MOVES = pltpu.CompilerParams(vmem_limit_bytes=16 * 1024 * 1024)
MOVED = pl.CostEstimate(flops=0, bytes_accessed=4 * 10**6, transcendentals=0)


def to_blocks(planes, count, part):
    return pl.pallas_call(
        pack_kernel,
        grid=(1,),
        in_specs=[pl.BlockSpec((count, 6, N, N), lambda step: (part, 0, 0, 0))],
        out_specs=pl.BlockSpec((32, 56 * count, 128), lambda step: (0, 0, 0)),
        out_shape=jax.ShapeDtypeStruct((32, 56 * count, 128), jnp.float32),
        scratch_shapes=[pltpu.VMEM((2, N, 128), jnp.float32)] * 2,
        compiler_params=PARAMS,
        cost_estimate=MOVED,
        name="pack",
    )(planes)


def in_parts(shape, dim, place):
    block = shape[:dim] + (shape[dim] // PARTS,) + shape[dim + 1 :]

    def part_place(part, step):
        at = place(step)
        return at[:dim] + (part,) + at[dim + 1 :]

    return [pl.BlockSpec(block, functools.partial(part_place, part)) for part in range(PARTS)]


def from_blocks(blocks):
    return pl.pallas_call(
        unpack_kernel,
        out_shape=jax.ShapeDtypeStruct((1, 6, N, N), jnp.float32),
        scratch_shapes=[pltpu.VMEM((2, N, 128), jnp.float32)] * 2,
        compiler_params=MOVES,
        cost_estimate=MOVED,
        name="unpack",
    )(blocks)


def by_slots(slots, spread):
    return pl.pallas_call(
        slots_kernel,
        in_specs=[pl.BlockSpec(memory_space=pltpu.SMEM), pl.BlockSpec(memory_space=pltpu.VMEM)],
        out_specs=[pl.BlockSpec(memory_space=pltpu.VMEM)] * 8,
        out_shape=[jax.ShapeDtypeStruct((24, LANES), jnp.float32)] * 8,
        compiler_params=MOVES,
        cost_estimate=MOVED,
        name="slots",
    )(slots, spread)


def choose(owner, spread):
    return pl.pallas_call(
        choose_kernel,
        grid_spec=pltpu.PrefetchScalarGridSpec(
            num_scalar_prefetch=1,
            grid=(2,),
            in_specs=[pl.BlockSpec((1, 4, 112, 128), lambda turn, owner: (owner[turn], 0, 0, 0))],
            out_specs=pl.BlockSpec((2, 24, LANES), lambda turn, owner: (turn, 0, 0)),
        ),
        out_shape=jax.ShapeDtypeStruct((4, 24, LANES), jnp.float32),
        compiler_params=MOVES,
        cost_estimate=MOVED,
        name="choose",
    )(owner, spread)


def forward(slots, pieces, bands):
    even, odd = lane_matrices()
    even, odd = lane_terms(even), lane_terms(odd)
    rows = stacked_terms(cas_matrix()[:, held_order()])
    return pl.pallas_call(
        forward_kernel,
        grid=(4,),
        in_specs=[
            pl.BlockSpec(memory_space=pltpu.SMEM),
            *[whole(piece) for piece in pieces],
            BANDS,
            whole(even),
            whole(odd),
            whole(rows),
        ],
        out_specs=SPECTRA,
        out_shape=jax.ShapeDtypeStruct((4, 8, TILES, 24, 128), jnp.float32),
        scratch_shapes=[pltpu.VMEM((8, 24, LANES), jnp.float32)],
        compiler_params=PARAMS,
        cost_estimate=COST,
        name="forward",
    )(slots, *pieces, bands, even, odd, rows)


def inverse(spectra, bands):
    even, odd = lane_matrices()
    even, odd = lane_terms(even), lane_terms(odd.T)
    rows = stacked_terms(cas_matrix()[held_order(), :])
    out = jax.ShapeDtypeStruct((8, 224, 128), jnp.float32)
    return pl.pallas_call(
        inverse_kernel,
        grid=(8,),
        in_specs=[
            *in_parts((1, 8, 1, TILES, 24, 128), 1, lambda step: (step % 4, 0, step // 4, 0, 0, 0)),
            *in_parts((8, 1, 24, LANES), 0, lambda step: (0, jnp.minimum(step, 3), 0, 0)),
            *in_parts((8, 1, 24, LANES), 0, lambda step: (0, jnp.maximum(step - 4, 0), 0, 0)),
            whole(even),
            whole(odd),
            whole(rows),
        ],
        out_specs=whole(out),
        out_shape=out,
        scratch_shapes=[pltpu.VMEM((N, LANES), jnp.float32)],
        compiler_params=pltpu.CompilerParams(vmem_limit_bytes=32 * 1024 * 1024),
        cost_estimate=COST,
        name="inverse",
    )(*[spectra] * PARTS, *[bands[0]] * PARTS, *[bands[1]] * PARTS, even, odd, rows)


def filtered(first, last, pair_wave, wave):
    to = stacked_terms(cas_matrix()[:, column_order()])
    back = stacked_terms(cas_matrix()[column_order(), :])
    block = (32, TILES, 8, 128)
    return pl.pallas_call(
        filter_kernel,
        grid=(6,),
        in_specs=[
            pl.BlockSpec(block, lambda step: (0, 0, jnp.minimum(step, 2), 0)),
            pl.BlockSpec(block, lambda step: (0, 0, jnp.maximum(step - 3, 0), 0)),
            pl.BlockSpec((1, 1, 8 * N), lambda step: (step % 3, 0, 0)),
            whole(wave),
            whole(to),
            whole(back),
        ],
        out_specs=pl.BlockSpec((32, 1, TILES, 8, 128), lambda step: (0, step // 3, 0, step % 3, 0)),
        out_shape=jax.ShapeDtypeStruct((32, 2, TILES, 24, 128), jnp.float32),
        compiler_params=pltpu.CompilerParams(vmem_limit_bytes=32 * 1024 * 1024),
        cost_estimate=COST,
        name="filter",
    )(first, last, pair_wave, wave, to, back)


def wavenumber(index):
    folded = jnp.minimum(index, N - index)
    return folded.astype(jnp.float32) * (2.0 * math.pi / N)


def filter_waves(place):
    wave = wavenumber(jnp.arange(N, dtype=jnp.int32)) ** 2
    mine = wavenumber((place % 8) * 24 + jnp.arange(24, dtype=jnp.int32)) ** 2
    screen = (4.0 * math.pi / N) ** 2
    pair = mine.reshape(3, 8, 1) + wave[None, None, :] + screen
    pair = jnp.concatenate([pair[:, :, :128].reshape(3, 1024), pair[:, :, 128:].reshape(3, 512)], axis=1)
    return pair.reshape(3, 1, 8 * N), wave.reshape(N, 1)


def exchange_plane(blocks):
    return lax.all_to_all(blocks, PLANE, 0, 0, tiled=True)


def exchange_z(blocks):
    return lax.all_to_all(blocks, "z", 0, 0, tiled=True)


SHIFTS = (0, 4, 3, 5, 2, 6, 1, 7)


def gather_orbital(spread, place):
    shifts = jnp.array(SHIFTS, jnp.int32)
    pieces = by_slots((place + shifts) % 8, spread)
    moved = [
        lax.ppermute(piece, "z", [(z, (z + shift) % 8) for z in range(8)])
        for piece, shift in zip(pieces[1:], SHIFTS[1:])
    ]
    return [pieces[0]] + moved, (place - shifts) % 8


def shards(resident, owned, owner):
    pair_wave, wave = filter_waves(lax.axis_index(PLANE))
    first = exchange_plane(to_blocks(owned[0], 2, 0))
    spread, first = lax.optimization_barrier((to_blocks(resident, 1, 0), first))
    halves = [lax.all_gather(choose(owner, first.reshape(8, 4, 112, 128)), "z", axis=0, tiled=False)]
    spread = exchange_plane(spread)
    second, spread = lax.optimization_barrier((to_blocks(owned[0], 2, 1), spread))
    orbital, slots = gather_orbital(spread.reshape(8, 4, 56, 128), lax.axis_index("z"))
    second, orbital = lax.optimization_barrier((exchange_plane(second), orbital))
    second = choose(owner, second.reshape(8, 4, 112, 128))
    halves.append(lax.all_gather(second, "z", axis=0, tiled=False))
    spectra = []
    for bands in halves:
        blocks = forward(slots, orbital, bands)
        blocks, pair_wave, wave = lax.optimization_barrier((blocks, pair_wave, wave))
        spectra.append(exchange_plane(blocks.reshape(32, 216, 128)).reshape(32, TILES, 24, 128))
    potentials = exchange_plane(filtered(*spectra, pair_wave, wave).reshape(32, 432, 128))
    total = inverse(potentials.reshape(4, 8, 2, TILES, 24, 128), halves)
    back = exchange_plane(exchange_z(total).reshape(32, 56, 128))
    return from_blocks(back)


def solution(mesh):
    fine = Mesh(mesh.devices.reshape(2, 4, 2, 8, 2), ("x_lo", "y", "x_hi", "z", "core"))
    band, slab = ("x_lo", "y"), ("x_hi", "z", "core")
    return jax.shard_map(
        shards,
        mesh=fine,
        in_specs=(P(band, slab), P(band, None, slab), P()),
        out_specs=P(band, slab),
        check_vma=False,
    )
```

```python
import math

import jax
import jax.numpy as jnp
import ml_dtypes
import numpy as np
from jax import lax
from jax.experimental import pallas as pl
from jax.experimental.pallas import tpu as pltpu
from jax.sharding import Mesh, PartitionSpec as P

N = 192
LANES = 6 * N
TILES = LANES // 128
PLANE = ("x_lo", "y", "x_hi", "core")
VMEM = 62 * 1024 * 1024


def cas_matrix():
    index = np.arange(N)
    phases = (index[:, None] * index[None, :] % N) * (2.0 * math.pi / N)
    return np.cos(phases) + np.sin(phases)


def held_order():
    z, x_hi, core, row = np.meshgrid(np.arange(8), np.arange(2), np.arange(2), np.arange(6), indexing="ij")
    return (6 * (x_hi * 16 + z * 2 + core) + row).reshape(-1)


def column_order():
    inner, device = np.meshgrid(np.arange(6), np.arange(32), indexing="ij")
    return (6 * device + inner).reshape(-1)


def two_terms(matrix):
    high = matrix.astype(np.float32).astype(ml_dtypes.bfloat16)
    low = (matrix - high.astype(np.float64)).astype(np.float32).astype(ml_dtypes.bfloat16)
    return np.stack([high, low])


def stacked_terms(matrix):
    high, low = two_terms(matrix)
    return jnp.asarray(np.concatenate([high, low, high], axis=1))


def lane_terms(matrix):
    high, low = two_terms(matrix)
    return jnp.asarray(np.concatenate([high, high, low], axis=0))


def lane_matrices():
    cas = cas_matrix()
    even, odd = np.zeros((256, 256)), np.zeros((256, 256))
    even[:N, :N] = cas
    odd[64:, 64:128] = cas[:, 128:]
    odd[64:, 128:] = cas[:, :128]
    return even, odd


def split(value):
    high = value.astype(jnp.bfloat16)
    return high, (value - high.astype(jnp.float32)).astype(jnp.bfloat16)


def dot(left, right):
    return jnp.dot(left, right, preferred_element_type=jnp.float32)


def left_product(matrix_ref, value):
    high, low = split(value)
    return dot(matrix_ref[...], jnp.concatenate([high, high, low], axis=0))


def right_product(high, low, matrix_ref):
    return dot(jnp.concatenate([high, low, high], axis=1), matrix_ref[...])


def lane_transform(value, even_ref, odd_ref):
    high, low = split(value)

    starts = range(0, value.shape[1], 384)

    def stacked(terms, offset):
        return jnp.concatenate([terms[:, s + offset : s + offset + 256] for s in starts], axis=0)

    first = right_product(stacked(high, 0), stacked(low, 0), even_ref)
    last = right_product(stacked(high, 128), stacked(low, 128), odd_ref)
    middle = first[:, 128:] + last[:, :128]
    tiles = []
    for start in range(0, len(starts) * N, N):
        for part in (first[:, :128], middle, last[:, 128:]):
            tiles.append(part[start : start + N])
    return jnp.concatenate(tiles, axis=1)


def pack_kernel(planes_ref, out_ref, left_ref, right_ref):
    fields, rows = planes_ref.shape[0], out_ref.shape[1]
    target = out_ref.reshape(32 * rows, 128)
    lower = lax.broadcasted_iota(jnp.int32, (32, 128), 1) < 64
    for field in range(fields):
        for a in range(6):
            slot = (6 * field + a) % 2
            left, right = left_ref.at[slot], right_ref.at[slot]
            left[...] = planes_ref[field, a, :, :128]
            right[:, :64] = planes_ref[field, a, :, 128:]
            for h in range(3):
                even, odd = pl.ds(2 * h, 32, stride=6), pl.ds(2 * h + 1, 32, stride=6)
                start = pltpu.roll(left[odd, :], 64, 1)
                end = pltpu.roll(right[odd, :], 64, 1)
                row = field * 54 + a * TILES + 3 * h
                target[pl.ds(row, 32, stride=rows), :] = left[even, :]
                target[pl.ds(row + 1, 32, stride=rows), :] = jnp.where(lower, right[even, :], start)
                target[pl.ds(row + 2, 32, stride=rows), :] = jnp.where(lower, start, end)


def slots_kernel(slots_ref, spread_ref, *out_refs):
    for slot, out_ref in enumerate(out_refs):
        for source in range(4):
            block = spread_ref.at[slots_ref[slot], source]
            for tile in range(TILES):
                rows = block[pl.ds(tile, 6, stride=TILES), :]
                out_ref[6 * source : 6 * source + 6, 128 * tile : 128 * tile + 128] = rows


def choose_kernel(owner_ref, spread_ref, out_ref):
    for source in range(4):
        block = spread_ref.at[0, source]
        for member in range(2):
            for tile in range(TILES):
                rows = block[pl.ds(54 * member + tile, 6, stride=TILES), :]
                out_ref[member, 6 * source : 6 * source + 6, 128 * tile : 128 * tile + 128] = rows


def forward_kernel(slots_ref, *refs):
    piece_refs, (band_ref, even_ref, odd_ref, rows_ref, out_ref, orbital_ref) = refs[:8], refs[8:]

    @pl.when(pl.program_id(0) == 0)
    def _():
        for slot, piece_ref in enumerate(piece_refs):
            orbital_ref[slots_ref[slot]] = piece_ref[...]

    pair = orbital_ref[...].reshape(N, LANES) * band_ref[:, 0].reshape(N, LANES)
    spectrum = lane_transform(pair, even_ref, odd_ref)
    spectrum = left_product(rows_ref, spectrum)
    for tile in range(TILES):
        out_ref[0, :, tile] = spectrum[:, 128 * tile : 128 * tile + 128].reshape(8, 24, 128)


def inverse_kernel(spectrum_ref, first_ref, last_ref, even_ref, odd_ref, rows_ref, out_ref, total_ref):
    step = pl.program_id(0)
    tiles = [spectrum_ref[pair, :, 0, tile].reshape(N, 128) for pair in range(2) for tile in range(TILES)]
    potential = left_product(rows_ref, jnp.concatenate(tiles, axis=1))
    potential = lane_transform(potential, even_ref, odd_ref)
    prefactor = -1.0 / math.sqrt(N * 8)
    weight = jnp.where(step % 2 == 0, prefactor, 2.0 * prefactor)

    def term(band_ref):
        one = band_ref[:, 0].reshape(N, LANES) * potential[:, :LANES]
        return weight * (one + band_ref[:, 1].reshape(N, LANES) * potential[:, LANES:])

    @pl.when(step == 0)
    def _():
        total_ref[...] = term(first_ref)

    @pl.when(step == 1)
    def _():
        total_ref[...] += term(first_ref)

    @pl.when(step >= 2)
    def _():
        total_ref[...] += term(last_ref)

    @pl.when(step == 3)
    def _():
        for z in range(8):
            for source in range(4):
                rows = pl.ds(24 * z + 6 * source, 6)
                for tile in range(TILES):
                    block = total_ref[rows, 128 * tile : 128 * tile + 128]
                    out_ref[z, 56 * source + 6 * tile : 56 * source + 6 * tile + 6, :] = block


def unpack_kernel(blocks_ref, out_ref, left_ref, right_ref):
    source = blocks_ref.reshape(32 * 56, 128)
    lower = lax.broadcasted_iota(jnp.int32, (32, 128), 1) < 64
    for a in range(6):
        left, right = left_ref.at[a % 2], right_ref.at[a % 2]
        for h in range(3):
            tiles = [source[pl.ds(18 * h + 6 * k + a, 32, stride=56), :] for k in range(3)]
            even, odd = pl.ds(2 * h, 32, stride=6), pl.ds(2 * h + 1, 32, stride=6)
            turned = pltpu.roll(tiles[2], 64, 1)
            left[even, :] = tiles[0]
            right[even, :] = tiles[1]
            left[odd, :] = jnp.where(lower, pltpu.roll(tiles[1], 64, 1), turned)
            right[odd, :] = turned
        out_ref[0, a, :, :128] = left[...]
        out_ref[0, a, :, 128:] = right[:, :64]


def filter_block(columns_ref, pair_ref, wave_ref, to_ref, from_ref, out_ref):
    source = columns_ref.reshape(32 * TILES * 8, 128)
    target = out_ref.reshape(32 * TILES * 8, 128)
    lower = lax.broadcasted_iota(jnp.int32, (32, 128), 1) < 64

    def rows(tile, k):
        return pl.ds(8 * tile + k, 32, stride=TILES * 8)

    blocks = []
    for k in range(8):
        tiles = [3 * (i // 2) + 2 * (i % 2) for i in range(6)]
        blocks.append(jnp.concatenate([source[rows(tile, k), :] for tile in tiles], axis=0))
    for k in range(0, 8, 2):
        parts = []
        for tile in (1, 4, 7):
            one, two = source[rows(tile, k), :], source[rows(tile, k + 1), :]
            parts.append(jnp.where(lower, one, pltpu.roll(two, 64, 1)))
            parts.append(jnp.where(lower, pltpu.roll(one, 64, 1), two))
        blocks.append(jnp.concatenate(parts, axis=0))
    columns = jnp.concatenate(blocks, axis=1)
    spectrum = left_product(to_ref, columns)
    spectrum = spectrum * ((4.0 * math.pi / float(N) ** 3) / (wave_ref[...] + pair_ref[0]))
    columns = left_product(from_ref, spectrum)
    for k in range(8):
        for i in range(6):
            tile = 3 * (i // 2) + 2 * (i % 2)
            target[rows(tile, k), :] = columns[32 * i : 32 * i + 32, 128 * k : 128 * k + 128]
    for k in range(0, 8, 2):
        start = 1024 + 64 * k
        for h in range(3):
            one = columns[64 * h : 64 * h + 32, start : start + 128]
            two = columns[64 * h + 32 : 64 * h + 64, start : start + 128]
            target[rows(3 * h + 1, k), :] = jnp.where(lower, one, pltpu.roll(two, 64, 1))
            target[rows(3 * h + 1, k + 1), :] = jnp.where(lower, pltpu.roll(one, 64, 1), two)


def filter_kernel(first_ref, last_ref, *refs):
    step = pl.program_id(0)

    @pl.when(step < 3)
    def _():
        filter_block(first_ref, *refs)

    @pl.when(step >= 3)
    def _():
        filter_block(last_ref, *refs)


def whole(array):
    return pl.BlockSpec(array.shape, lambda step: (0,) * len(array.shape))


PARAMS = pltpu.CompilerParams(vmem_limit_bytes=VMEM)
COST = pl.CostEstimate(flops=16 * 10**9, bytes_accessed=10**7, transcendentals=0)
BANDS = pl.BlockSpec((8, 1, 24, LANES), lambda step: (0, step, 0, 0))
SPECTRA = pl.BlockSpec((1, 8, TILES, 24, 128), lambda step: (step, 0, 0, 0, 0))


MOVES = pltpu.CompilerParams(vmem_limit_bytes=16 * 1024 * 1024)
MOVED = pl.CostEstimate(flops=0, bytes_accessed=4 * 10**6, transcendentals=0)


def to_blocks(planes, count, part):
    return pl.pallas_call(
        pack_kernel,
        grid=(1,),
        in_specs=[pl.BlockSpec((count, 6, N, N), lambda step: (part, 0, 0, 0))],
        out_specs=pl.BlockSpec((32, 56 * count, 128), lambda step: (0, 0, 0)),
        out_shape=jax.ShapeDtypeStruct((32, 56 * count, 128), jnp.float32),
        scratch_shapes=[pltpu.VMEM((2, N, 128), jnp.float32)] * 2,
        compiler_params=PARAMS,
        cost_estimate=MOVED,
        name="pack",
    )(planes)


def from_blocks(blocks):
    return pl.pallas_call(
        unpack_kernel,
        out_shape=jax.ShapeDtypeStruct((1, 6, N, N), jnp.float32),
        scratch_shapes=[pltpu.VMEM((2, N, 128), jnp.float32)] * 2,
        compiler_params=MOVES,
        cost_estimate=MOVED,
        name="unpack",
    )(blocks)


def by_slots(slots, spread):
    return pl.pallas_call(
        slots_kernel,
        in_specs=[pl.BlockSpec(memory_space=pltpu.SMEM), pl.BlockSpec(memory_space=pltpu.VMEM)],
        out_specs=[pl.BlockSpec(memory_space=pltpu.VMEM)] * 8,
        out_shape=[jax.ShapeDtypeStruct((24, LANES), jnp.float32)] * 8,
        compiler_params=MOVES,
        cost_estimate=MOVED,
        name="slots",
    )(slots, spread)


def choose(owner, spread):
    return pl.pallas_call(
        choose_kernel,
        grid_spec=pltpu.PrefetchScalarGridSpec(
            num_scalar_prefetch=1,
            grid=(2,),
            in_specs=[pl.BlockSpec((1, 4, 112, 128), lambda turn, owner: (owner[turn], 0, 0, 0))],
            out_specs=pl.BlockSpec((2, 24, LANES), lambda turn, owner: (turn, 0, 0)),
        ),
        out_shape=jax.ShapeDtypeStruct((4, 24, LANES), jnp.float32),
        compiler_params=MOVES,
        cost_estimate=MOVED,
        name="choose",
    )(owner, spread)


def forward(slots, pieces, bands):
    even, odd = lane_matrices()
    even, odd = lane_terms(even), lane_terms(odd)
    rows = stacked_terms(cas_matrix()[:, held_order()])
    return pl.pallas_call(
        forward_kernel,
        grid=(4,),
        in_specs=[
            pl.BlockSpec(memory_space=pltpu.SMEM),
            *[whole(piece) for piece in pieces],
            BANDS,
            whole(even),
            whole(odd),
            whole(rows),
        ],
        out_specs=SPECTRA,
        out_shape=jax.ShapeDtypeStruct((4, 8, TILES, 24, 128), jnp.float32),
        scratch_shapes=[pltpu.VMEM((8, 24, LANES), jnp.float32)],
        compiler_params=PARAMS,
        cost_estimate=COST,
        name="forward",
    )(slots, *pieces, bands, even, odd, rows)


def inverse(spectra, bands):
    even, odd = lane_matrices()
    even, odd = lane_terms(even), lane_terms(odd.T)
    rows = stacked_terms(cas_matrix()[held_order(), :])
    out = jax.ShapeDtypeStruct((8, 224, 128), jnp.float32)
    return pl.pallas_call(
        inverse_kernel,
        grid=(4,),
        in_specs=[
            pl.BlockSpec((2, 8, 1, TILES, 24, 128), lambda step: (step % 2, 0, step // 2, 0, 0, 0)),
            pl.BlockSpec((8, 2, 24, LANES), lambda step: (0, jnp.minimum(step, 1), 0, 0)),
            pl.BlockSpec((8, 2, 24, LANES), lambda step: (0, jnp.maximum(step - 2, 0), 0, 0)),
            whole(even),
            whole(odd),
            whole(rows),
        ],
        out_specs=whole(out),
        out_shape=out,
        scratch_shapes=[pltpu.VMEM((N, LANES), jnp.float32)],
        compiler_params=pltpu.CompilerParams(vmem_limit_bytes=32 * 1024 * 1024),
        cost_estimate=COST,
        name="inverse",
    )(spectra, *bands, even, odd, rows)


def filtered(first, last, pair_wave, wave):
    to = stacked_terms(cas_matrix()[:, column_order()])
    back = stacked_terms(cas_matrix()[column_order(), :])
    block = (32, TILES, 8, 128)
    return pl.pallas_call(
        filter_kernel,
        grid=(6,),
        in_specs=[
            pl.BlockSpec(block, lambda step: (0, 0, jnp.minimum(step, 2), 0)),
            pl.BlockSpec(block, lambda step: (0, 0, jnp.maximum(step - 3, 0), 0)),
            pl.BlockSpec((1, 1, 8 * N), lambda step: (step % 3, 0, 0)),
            whole(wave),
            whole(to),
            whole(back),
        ],
        out_specs=pl.BlockSpec((32, 1, TILES, 8, 128), lambda step: (0, step // 3, 0, step % 3, 0)),
        out_shape=jax.ShapeDtypeStruct((32, 2, TILES, 24, 128), jnp.float32),
        compiler_params=pltpu.CompilerParams(vmem_limit_bytes=32 * 1024 * 1024),
        cost_estimate=COST,
        name="filter",
    )(first, last, pair_wave, wave, to, back)


def wavenumber(index):
    folded = jnp.minimum(index, N - index)
    return folded.astype(jnp.float32) * (2.0 * math.pi / N)


def filter_waves(place):
    wave = wavenumber(jnp.arange(N, dtype=jnp.int32)) ** 2
    mine = wavenumber((place % 8) * 24 + jnp.arange(24, dtype=jnp.int32)) ** 2
    screen = (4.0 * math.pi / N) ** 2
    pair = mine.reshape(3, 8, 1) + wave[None, None, :] + screen
    pair = jnp.concatenate([pair[:, :, :128].reshape(3, 1024), pair[:, :, 128:].reshape(3, 512)], axis=1)
    return pair.reshape(3, 1, 8 * N), wave.reshape(N, 1)


def exchange_plane(blocks):
    return lax.all_to_all(blocks, PLANE, 0, 0, tiled=True)


def exchange_z(blocks):
    return lax.all_to_all(blocks, "z", 0, 0, tiled=True)


SHIFTS = (0, 4, 3, 5, 2, 6, 1, 7)


def gather_orbital(spread, place):
    shifts = jnp.array(SHIFTS, jnp.int32)
    pieces = by_slots((place + shifts) % 8, spread)
    moved = [
        lax.ppermute(piece, "z", [(z, (z + shift) % 8) for z in range(8)])
        for piece, shift in zip(pieces[1:], SHIFTS[1:])
    ]
    return [pieces[0]] + moved, (place - shifts) % 8


def shards(resident, owned, owner):
    pair_wave, wave = filter_waves(lax.axis_index(PLANE))
    first = exchange_plane(to_blocks(owned[0], 2, 0))
    spread, first = lax.optimization_barrier((to_blocks(resident, 1, 0), first))
    halves = [lax.all_gather(choose(owner, first.reshape(8, 4, 112, 128)), "z", axis=0, tiled=False)]
    spread = exchange_plane(spread)
    second, spread = lax.optimization_barrier((to_blocks(owned[0], 2, 1), spread))
    orbital, slots = gather_orbital(spread.reshape(8, 4, 56, 128), lax.axis_index("z"))
    second, orbital = lax.optimization_barrier((exchange_plane(second), orbital))
    second = choose(owner, second.reshape(8, 4, 112, 128))
    halves.append(lax.all_gather(second, "z", axis=0, tiled=False))
    spectra = []
    for bands in halves:
        blocks = forward(slots, orbital, bands)
        blocks, pair_wave, wave = lax.optimization_barrier((blocks, pair_wave, wave))
        spectra.append(exchange_plane(blocks.reshape(32, 216, 128)).reshape(32, TILES, 24, 128))
    potentials = exchange_plane(filtered(*spectra, pair_wave, wave).reshape(32, 432, 128))
    total = inverse(potentials.reshape(4, 8, 2, TILES, 24, 128), halves)
    back = exchange_plane(exchange_z(total).reshape(32, 56, 128))
    return from_blocks(back)


def solution(mesh):
    fine = Mesh(mesh.devices.reshape(2, 4, 2, 8, 2), ("x_lo", "y", "x_hi", "z", "core"))
    band, slab = ("x_lo", "y"), ("x_hi", "z", "core")
    return jax.shard_map(
        shards,
        mesh=fine,
        in_specs=(P(band, slab), P(band, None, slab), P()),
        out_specs=P(band, slab),
        check_vma=False,
    )
```

```python
import math

import jax
import jax.numpy as jnp
import ml_dtypes
import numpy as np
from jax import lax
from jax.experimental import pallas as pl
from jax.experimental.pallas import tpu as pltpu
from jax.sharding import Mesh, PartitionSpec as P

N = 192
LANES = 6 * N
TILES = LANES // 128
PLANE = ("x_lo", "y", "x_hi", "core")
VMEM = 62 * 1024 * 1024


def cas_matrix():
    index = np.arange(N)
    phases = (index[:, None] * index[None, :] % N) * (2.0 * math.pi / N)
    return np.cos(phases) + np.sin(phases)


def held_order():
    z, x_hi, core, row = np.meshgrid(np.arange(8), np.arange(2), np.arange(2), np.arange(6), indexing="ij")
    return (6 * (x_hi * 16 + z * 2 + core) + row).reshape(-1)


def column_order():
    inner, device = np.meshgrid(np.arange(6), np.arange(32), indexing="ij")
    return (6 * device + inner).reshape(-1)


def two_terms(matrix):
    high = matrix.astype(np.float32).astype(ml_dtypes.bfloat16)
    low = (matrix - high.astype(np.float64)).astype(np.float32).astype(ml_dtypes.bfloat16)
    return np.stack([high, low])


def stacked_terms(matrix):
    high, low = two_terms(matrix)
    return jnp.asarray(np.concatenate([high, low, high], axis=1))


def lane_terms(matrix):
    high, low = two_terms(matrix)
    return jnp.asarray(np.concatenate([high, high, low], axis=0))


def lane_matrices():
    cas = cas_matrix()
    even, odd = np.zeros((256, 256)), np.zeros((256, 256))
    even[:N, :N] = cas
    odd[64:, 64:128] = cas[:, 128:]
    odd[64:, 128:] = cas[:, :128]
    return even, odd


def split(value):
    high = value.astype(jnp.bfloat16)
    return high, (value - high.astype(jnp.float32)).astype(jnp.bfloat16)


def dot(left, right):
    return jnp.dot(left, right, preferred_element_type=jnp.float32)


def left_product(matrix_ref, value):
    high, low = split(value)
    return dot(matrix_ref[...], jnp.concatenate([high, high, low], axis=0))


def right_product(high, low, matrix_ref):
    return dot(jnp.concatenate([high, low, high], axis=1), matrix_ref[...])


def lane_transform(value, even_ref, odd_ref):
    high, low = split(value)

    starts = range(0, value.shape[1], 384)

    def stacked(terms, offset):
        return jnp.concatenate([terms[:, s + offset : s + offset + 256] for s in starts], axis=0)

    first = right_product(stacked(high, 0), stacked(low, 0), even_ref)
    last = right_product(stacked(high, 128), stacked(low, 128), odd_ref)
    middle = first[:, 128:] + last[:, :128]
    tiles = []
    for start in range(0, len(starts) * N, N):
        for part in (first[:, :128], middle, last[:, 128:]):
            tiles.append(part[start : start + N])
    return jnp.concatenate(tiles, axis=1)


def pack_kernel(planes_ref, out_ref, left_ref, right_ref):
    fields, rows = planes_ref.shape[0], out_ref.shape[1]
    target = out_ref.reshape(32 * rows, 128)
    lower = lax.broadcasted_iota(jnp.int32, (32, 128), 1) < 64
    for field in range(fields):
        for a in range(6):
            slot = (6 * field + a) % 2
            left, right = left_ref.at[slot], right_ref.at[slot]
            left[...] = planes_ref[field, a, :, :128]
            right[:, :64] = planes_ref[field, a, :, 128:]
            for h in range(3):
                even, odd = pl.ds(2 * h, 32, stride=6), pl.ds(2 * h + 1, 32, stride=6)
                start = pltpu.roll(left[odd, :], 64, 1)
                end = pltpu.roll(right[odd, :], 64, 1)
                row = field * 54 + a * TILES + 3 * h
                target[pl.ds(row, 32, stride=rows), :] = left[even, :]
                target[pl.ds(row + 1, 32, stride=rows), :] = jnp.where(lower, right[even, :], start)
                target[pl.ds(row + 2, 32, stride=rows), :] = jnp.where(lower, start, end)


def slots_kernel(slots_ref, spread_ref, *out_refs):
    for slot, out_ref in enumerate(out_refs):
        for source in range(4):
            block = spread_ref.at[slots_ref[slot], source]
            for tile in range(TILES):
                rows = block[pl.ds(tile, 6, stride=TILES), :]
                out_ref[6 * source : 6 * source + 6, 128 * tile : 128 * tile + 128] = rows


def choose_kernel(owner_ref, spread_ref, out_ref):
    for source in range(4):
        block = spread_ref.at[0, source]
        for member in range(2):
            for tile in range(TILES):
                rows = block[pl.ds(54 * member + tile, 6, stride=TILES), :]
                out_ref[member, 6 * source : 6 * source + 6, 128 * tile : 128 * tile + 128] = rows


def forward_kernel(slots_ref, *refs):
    piece_refs, (band_ref, even_ref, odd_ref, rows_ref, out_ref, orbital_ref) = refs[:8], refs[8:]

    @pl.when(pl.program_id(0) == 0)
    def _():
        for slot, piece_ref in enumerate(piece_refs):
            orbital_ref[slots_ref[slot]] = piece_ref[...]

    pair = orbital_ref[...].reshape(N, LANES) * band_ref[:, 0].reshape(N, LANES)
    spectrum = lane_transform(pair, even_ref, odd_ref)
    spectrum = left_product(rows_ref, spectrum)
    for tile in range(TILES):
        out_ref[0, :, tile] = spectrum[:, 128 * tile : 128 * tile + 128].reshape(8, 24, 128)


def inverse_kernel(spectrum_ref, first_ref, last_ref, even_ref, odd_ref, rows_ref, out_ref, total_ref):
    step = pl.program_id(0)
    tiles = [spectrum_ref[pair, :, 0, tile].reshape(N, 128) for pair in range(2) for tile in range(TILES)]
    potential = left_product(rows_ref, jnp.concatenate(tiles, axis=1))
    potential = lane_transform(potential, even_ref, odd_ref)
    prefactor = -1.0 / math.sqrt(N * 8)
    weight = jnp.where(step % 2 == 0, prefactor, 2.0 * prefactor)

    def term(band_ref):
        one = band_ref[:, 0].reshape(N, LANES) * potential[:, :LANES]
        return weight * (one + band_ref[:, 1].reshape(N, LANES) * potential[:, LANES:])

    @pl.when(step == 0)
    def _():
        total_ref[...] = term(first_ref)

    @pl.when(step == 1)
    def _():
        total_ref[...] += term(first_ref)

    @pl.when(step >= 2)
    def _():
        total_ref[...] += term(last_ref)

    @pl.when(step == 3)
    def _():
        for z in range(8):
            for source in range(4):
                rows = pl.ds(24 * z + 6 * source, 6)
                for tile in range(TILES):
                    block = total_ref[rows, 128 * tile : 128 * tile + 128]
                    out_ref[z, 56 * source + 6 * tile : 56 * source + 6 * tile + 6, :] = block


def unpack_kernel(blocks_ref, out_ref, left_ref, right_ref):
    source = blocks_ref.reshape(32 * 56, 128)
    lower = lax.broadcasted_iota(jnp.int32, (32, 128), 1) < 64
    for a in range(6):
        left, right = left_ref.at[a % 2], right_ref.at[a % 2]
        for h in range(3):
            tiles = [source[pl.ds(18 * h + 6 * k + a, 32, stride=56), :] for k in range(3)]
            even, odd = pl.ds(2 * h, 32, stride=6), pl.ds(2 * h + 1, 32, stride=6)
            turned = pltpu.roll(tiles[2], 64, 1)
            left[even, :] = tiles[0]
            right[even, :] = tiles[1]
            left[odd, :] = jnp.where(lower, pltpu.roll(tiles[1], 64, 1), turned)
            right[odd, :] = turned
        out_ref[0, a, :, :128] = left[...]
        out_ref[0, a, :, 128:] = right[:, :64]


def filter_block(columns_ref, to_ref, from_ref, out_ref, coulomb_ref):
    source = columns_ref.reshape(32 * TILES * 8, 128)
    target = out_ref.reshape(32 * TILES * 8, 128)
    lower = lax.broadcasted_iota(jnp.int32, (32, 128), 1) < 64

    def rows(tile, k):
        return pl.ds(8 * tile + k, 32, stride=TILES * 8)

    blocks = []
    for k in range(8):
        tiles = [3 * (i // 2) + 2 * (i % 2) for i in range(6)]
        blocks.append(jnp.concatenate([source[rows(tile, k), :] for tile in tiles], axis=0))
    for k in range(0, 8, 2):
        parts = []
        for tile in (1, 4, 7):
            one, two = source[rows(tile, k), :], source[rows(tile, k + 1), :]
            parts.append(jnp.where(lower, one, pltpu.roll(two, 64, 1)))
            parts.append(jnp.where(lower, pltpu.roll(one, 64, 1), two))
        blocks.append(jnp.concatenate(parts, axis=0))
    columns = jnp.concatenate(blocks, axis=1)
    spectrum = left_product(to_ref, columns)
    spectrum = spectrum * coulomb_ref[...]
    columns = left_product(from_ref, spectrum)
    for k in range(8):
        for i in range(6):
            tile = 3 * (i // 2) + 2 * (i % 2)
            target[rows(tile, k), :] = columns[32 * i : 32 * i + 32, 128 * k : 128 * k + 128]
    for k in range(0, 8, 2):
        start = 1024 + 64 * k
        for h in range(3):
            one = columns[64 * h : 64 * h + 32, start : start + 128]
            two = columns[64 * h + 32 : 64 * h + 64, start : start + 128]
            target[rows(3 * h + 1, k), :] = jnp.where(lower, one, pltpu.roll(two, 64, 1))
            target[rows(3 * h + 1, k + 1), :] = jnp.where(lower, pltpu.roll(one, 64, 1), two)


def filter_kernel(first_ref, last_ref, pair_ref, wave_ref, *refs):
    coulomb_ref = refs[-1]
    half = pl.program_id(0) % 2

    @pl.when(half == 0)
    def _():
        coulomb_ref[...] = (4.0 * math.pi / float(N) ** 3) / (wave_ref[...] + pair_ref[0])
        filter_block(first_ref, *refs)

    @pl.when(half == 1)
    def _():
        filter_block(last_ref, *refs)


def whole(array):
    return pl.BlockSpec(array.shape, lambda step: (0,) * len(array.shape))


PARAMS = pltpu.CompilerParams(vmem_limit_bytes=VMEM)
COST = pl.CostEstimate(flops=16 * 10**9, bytes_accessed=10**7, transcendentals=0)
BANDS = pl.BlockSpec((8, 1, 24, LANES), lambda step: (0, step, 0, 0))
SPECTRA = pl.BlockSpec((1, 8, TILES, 24, 128), lambda step: (step, 0, 0, 0, 0))


MOVES = pltpu.CompilerParams(vmem_limit_bytes=16 * 1024 * 1024)
MOVED = pl.CostEstimate(flops=0, bytes_accessed=4 * 10**6, transcendentals=0)


def to_blocks(planes, count, part):
    return pl.pallas_call(
        pack_kernel,
        grid=(1,),
        in_specs=[pl.BlockSpec((count, 6, N, N), lambda step: (part, 0, 0, 0))],
        out_specs=pl.BlockSpec((32, 56 * count, 128), lambda step: (0, 0, 0)),
        out_shape=jax.ShapeDtypeStruct((32, 56 * count, 128), jnp.float32),
        scratch_shapes=[pltpu.VMEM((2, N, 128), jnp.float32)] * 2,
        compiler_params=PARAMS,
        cost_estimate=MOVED,
        name="pack",
    )(planes)


def from_blocks(blocks):
    return pl.pallas_call(
        unpack_kernel,
        out_shape=jax.ShapeDtypeStruct((1, 6, N, N), jnp.float32),
        scratch_shapes=[pltpu.VMEM((2, N, 128), jnp.float32)] * 2,
        compiler_params=MOVES,
        cost_estimate=MOVED,
        name="unpack",
    )(blocks)


def by_slots(slots, spread):
    return pl.pallas_call(
        slots_kernel,
        in_specs=[pl.BlockSpec(memory_space=pltpu.SMEM), pl.BlockSpec(memory_space=pltpu.VMEM)],
        out_specs=[pl.BlockSpec(memory_space=pltpu.VMEM)] * 8,
        out_shape=[jax.ShapeDtypeStruct((24, LANES), jnp.float32)] * 8,
        compiler_params=MOVES,
        cost_estimate=MOVED,
        name="slots",
    )(slots, spread)


def choose(owner, spread):
    return pl.pallas_call(
        choose_kernel,
        grid_spec=pltpu.PrefetchScalarGridSpec(
            num_scalar_prefetch=1,
            grid=(2,),
            in_specs=[pl.BlockSpec((1, 4, 112, 128), lambda turn, owner: (owner[turn], 0, 0, 0))],
            out_specs=pl.BlockSpec((2, 24, LANES), lambda turn, owner: (turn, 0, 0)),
        ),
        out_shape=jax.ShapeDtypeStruct((4, 24, LANES), jnp.float32),
        compiler_params=MOVES,
        cost_estimate=MOVED,
        name="choose",
    )(owner, spread)


def forward(slots, pieces, bands):
    even, odd = lane_matrices()
    even, odd = lane_terms(even), lane_terms(odd)
    rows = stacked_terms(cas_matrix()[:, held_order()])
    return pl.pallas_call(
        forward_kernel,
        grid=(4,),
        in_specs=[
            pl.BlockSpec(memory_space=pltpu.SMEM),
            *[whole(piece) for piece in pieces],
            BANDS,
            whole(even),
            whole(odd),
            whole(rows),
        ],
        out_specs=SPECTRA,
        out_shape=jax.ShapeDtypeStruct((4, 8, TILES, 24, 128), jnp.float32),
        scratch_shapes=[pltpu.VMEM((8, 24, LANES), jnp.float32)],
        compiler_params=PARAMS,
        cost_estimate=COST,
        name="forward",
    )(slots, *pieces, bands, even, odd, rows)


def inverse(spectra, bands):
    even, odd = lane_matrices()
    even, odd = lane_terms(even), lane_terms(odd.T)
    rows = stacked_terms(cas_matrix()[held_order(), :])
    out = jax.ShapeDtypeStruct((8, 224, 128), jnp.float32)
    return pl.pallas_call(
        inverse_kernel,
        grid=(4,),
        in_specs=[
            pl.BlockSpec((2, 8, 1, TILES, 24, 128), lambda step: (step % 2, 0, step // 2, 0, 0, 0)),
            pl.BlockSpec((8, 2, 24, LANES), lambda step: (0, jnp.minimum(step, 1), 0, 0)),
            pl.BlockSpec((8, 2, 24, LANES), lambda step: (0, jnp.maximum(step - 2, 0), 0, 0)),
            whole(even),
            whole(odd),
            whole(rows),
        ],
        out_specs=whole(out),
        out_shape=out,
        scratch_shapes=[pltpu.VMEM((N, LANES), jnp.float32)],
        compiler_params=pltpu.CompilerParams(vmem_limit_bytes=32 * 1024 * 1024),
        cost_estimate=COST,
        name="inverse",
    )(spectra, *bands, even, odd, rows)


def filtered(first, last, pair_wave, wave):
    to = stacked_terms(cas_matrix()[:, column_order()])
    back = stacked_terms(cas_matrix()[column_order(), :])
    block = (32, TILES, 8, 128)
    return pl.pallas_call(
        filter_kernel,
        grid=(6,),
        in_specs=[
            pl.BlockSpec(block, lambda step: (0, 0, step // 2, 0)),
            pl.BlockSpec(block, lambda step: (0, 0, step // 2, 0)),
            pl.BlockSpec((1, 1, 8 * N), lambda step: (step // 2, 0, 0)),
            whole(wave),
            whole(to),
            whole(back),
        ],
        out_specs=pl.BlockSpec((32, 1, TILES, 8, 128), lambda step: (0, step % 2, 0, step // 2, 0)),
        out_shape=jax.ShapeDtypeStruct((32, 2, TILES, 24, 128), jnp.float32),
        scratch_shapes=[pltpu.VMEM((N, 8 * N), jnp.float32)],
        compiler_params=pltpu.CompilerParams(vmem_limit_bytes=32 * 1024 * 1024),
        cost_estimate=COST,
        name="filter",
    )(first, last, pair_wave, wave, to, back)


def wavenumber(index):
    folded = jnp.minimum(index, N - index)
    return folded.astype(jnp.float32) * (2.0 * math.pi / N)


def filter_waves(place):
    wave = wavenumber(jnp.arange(N, dtype=jnp.int32)) ** 2
    mine = wavenumber((place % 8) * 24 + jnp.arange(24, dtype=jnp.int32)) ** 2
    screen = (4.0 * math.pi / N) ** 2
    pair = mine.reshape(3, 8, 1) + wave[None, None, :] + screen
    pair = jnp.concatenate([pair[:, :, :128].reshape(3, 1024), pair[:, :, 128:].reshape(3, 512)], axis=1)
    return pair.reshape(3, 1, 8 * N), wave.reshape(N, 1)


def exchange_plane(blocks):
    return lax.all_to_all(blocks, PLANE, 0, 0, tiled=True)


def exchange_z(blocks):
    return lax.all_to_all(blocks, "z", 0, 0, tiled=True)


SHIFTS = (0, 4, 3, 5, 2, 6, 1, 7)


def gather_orbital(spread, place):
    shifts = jnp.array(SHIFTS, jnp.int32)
    pieces = by_slots((place + shifts) % 8, spread)
    moved = [
        lax.ppermute(piece, "z", [(z, (z + shift) % 8) for z in range(8)])
        for piece, shift in zip(pieces[1:], SHIFTS[1:])
    ]
    return [pieces[0]] + moved, (place - shifts) % 8


def shards(resident, owned, owner):
    pair_wave, wave = filter_waves(lax.axis_index(PLANE))
    first = exchange_plane(to_blocks(owned[0], 2, 0))
    spread, first = lax.optimization_barrier((to_blocks(resident, 1, 0), first))
    halves = [lax.all_gather(choose(owner, first.reshape(8, 4, 112, 128)), "z", axis=0, tiled=False)]
    spread = exchange_plane(spread)
    second, spread = lax.optimization_barrier((to_blocks(owned[0], 2, 1), spread))
    orbital, slots = gather_orbital(spread.reshape(8, 4, 56, 128), lax.axis_index("z"))
    second, orbital = lax.optimization_barrier((exchange_plane(second), orbital))
    second = choose(owner, second.reshape(8, 4, 112, 128))
    halves.append(lax.all_gather(second, "z", axis=0, tiled=False))
    spectra = []
    for bands in halves:
        blocks = forward(slots, orbital, bands)
        blocks, pair_wave, wave = lax.optimization_barrier((blocks, pair_wave, wave))
        spectra.append(exchange_plane(blocks.reshape(32, 216, 128)).reshape(32, TILES, 24, 128))
    potentials = exchange_plane(filtered(*spectra, pair_wave, wave).reshape(32, 432, 128))
    total = inverse(potentials.reshape(4, 8, 2, TILES, 24, 128), halves)
    back = exchange_plane(exchange_z(total).reshape(32, 56, 128))
    return from_blocks(back)


def solution(mesh):
    fine = Mesh(mesh.devices.reshape(2, 4, 2, 8, 2), ("x_lo", "y", "x_hi", "z", "core"))
    band, slab = ("x_lo", "y"), ("x_hi", "z", "core")
    return jax.shard_map(
        shards,
        mesh=fine,
        in_specs=(P(band, slab), P(band, None, slab), P()),
        out_specs=P(band, slab),
        check_vma=False,
    )
```

```python
import math

import jax
import jax.numpy as jnp
import ml_dtypes
import numpy as np
from jax import lax
from jax.experimental import pallas as pl
from jax.experimental.pallas import tpu as pltpu
from jax.sharding import Mesh, PartitionSpec as P

N = 192
LANES = 6 * N
TILES = LANES // 128
PLANE = ("x_lo", "y", "x_hi", "core")
VMEM = 62 * 1024 * 1024


def cas_matrix():
    index = np.arange(N)
    phases = (index[:, None] * index[None, :] % N) * (2.0 * math.pi / N)
    return np.cos(phases) + np.sin(phases)


def held_order():
    z, x_hi, core, row = np.meshgrid(np.arange(8), np.arange(2), np.arange(2), np.arange(6), indexing="ij")
    return (6 * (x_hi * 16 + z * 2 + core) + row).reshape(-1)


def column_order():
    inner, device = np.meshgrid(np.arange(6), np.arange(32), indexing="ij")
    return (6 * device + inner).reshape(-1)


def two_terms(matrix):
    high = matrix.astype(np.float32).astype(ml_dtypes.bfloat16)
    low = (matrix - high.astype(np.float64)).astype(np.float32).astype(ml_dtypes.bfloat16)
    return np.stack([high, low])


def stacked_terms(matrix):
    high, low = two_terms(matrix)
    return jnp.asarray(np.concatenate([high, low, high], axis=1))


def lane_terms(matrix):
    high, low = two_terms(matrix)
    return jnp.asarray(np.concatenate([high, high, low], axis=0))


def lane_matrices():
    cas = cas_matrix()
    even, odd = np.zeros((256, 256)), np.zeros((256, 256))
    even[:N, :N] = cas
    odd[64:, 64:128] = cas[:, 128:]
    odd[64:, 128:] = cas[:, :128]
    return even, odd


def split(value):
    high = value.astype(jnp.bfloat16)
    return high, (value - high.astype(jnp.float32)).astype(jnp.bfloat16)


def dot(left, right):
    return jnp.dot(left, right, preferred_element_type=jnp.float32)


def left_product(matrix_ref, value):
    high, low = split(value)
    return dot(matrix_ref[...], jnp.concatenate([high, high, low], axis=0))


def right_product(high, low, matrix_ref):
    return dot(jnp.concatenate([high, low, high], axis=1), matrix_ref[...])


def lane_transform(value, even_ref, odd_ref):
    high, low = split(value)

    starts = range(0, value.shape[1], 384)

    def stacked(terms, offset):
        return jnp.concatenate([terms[:, s + offset : s + offset + 256] for s in starts], axis=0)

    first = right_product(stacked(high, 0), stacked(low, 0), even_ref)
    last = right_product(stacked(high, 128), stacked(low, 128), odd_ref)
    middle = first[:, 128:] + last[:, :128]
    tiles = []
    for start in range(0, len(starts) * N, N):
        for part in (first[:, :128], middle, last[:, 128:]):
            tiles.append(part[start : start + N])
    return jnp.concatenate(tiles, axis=1)


def pack_kernel(planes_ref, out_ref, left_ref, right_ref):
    fields, rows = planes_ref.shape[0], out_ref.shape[1]
    target = out_ref.reshape(32 * rows, 128)
    lower = lax.broadcasted_iota(jnp.int32, (32, 128), 1) < 64
    for field in range(fields):
        for a in range(6):
            slot = (6 * field + a) % 2
            left, right = left_ref.at[slot], right_ref.at[slot]
            left[...] = planes_ref[field, a, :, :128]
            right[:, :64] = planes_ref[field, a, :, 128:]
            for h in range(3):
                even, odd = pl.ds(2 * h, 32, stride=6), pl.ds(2 * h + 1, 32, stride=6)
                start = pltpu.roll(left[odd, :], 64, 1)
                end = pltpu.roll(right[odd, :], 64, 1)
                row = field * 54 + a * TILES + 3 * h
                target[pl.ds(row, 32, stride=rows), :] = left[even, :]
                target[pl.ds(row + 1, 32, stride=rows), :] = jnp.where(lower, right[even, :], start)
                target[pl.ds(row + 2, 32, stride=rows), :] = jnp.where(lower, start, end)


def slots_kernel(slots_ref, spread_ref, *out_refs):
    for slot, out_ref in enumerate(out_refs):
        for source in range(4):
            block = spread_ref.at[slots_ref[slot], source]
            for tile in range(TILES):
                rows = block[pl.ds(tile, 6, stride=TILES), :]
                out_ref[6 * source : 6 * source + 6, 128 * tile : 128 * tile + 128] = rows


def choose_kernel(owner_ref, spread_ref, out_ref):
    for source in range(4):
        block = spread_ref.at[0, source]
        for member in range(2):
            for tile in range(TILES):
                rows = block[pl.ds(54 * member + tile, 6, stride=TILES), :]
                out_ref[member, 6 * source : 6 * source + 6, 128 * tile : 128 * tile + 128] = rows


def forward_kernel(slots_ref, *refs):
    piece_refs, (band_ref, even_ref, odd_ref, rows_ref, out_ref, orbital_ref) = refs[:8], refs[8:]

    @pl.when(pl.program_id(0) == 0)
    def _():
        for slot, piece_ref in enumerate(piece_refs):
            orbital_ref[slots_ref[slot]] = piece_ref[...]

    orbital = orbital_ref[...].reshape(N, LANES)
    pairs = [orbital * band_ref[:, pair].reshape(N, LANES) for pair in range(2)]
    spectrum = lane_transform(jnp.concatenate(pairs, axis=1), even_ref, odd_ref)
    spectrum = left_product(rows_ref, spectrum)
    for pair in range(2):
        for tile in range(TILES):
            start = LANES * pair + 128 * tile
            out_ref[pair, :, tile] = spectrum[:, start : start + 128].reshape(8, 24, 128)


def inverse_kernel(spectrum_ref, first_ref, last_ref, even_ref, odd_ref, rows_ref, out_ref, total_ref):
    step = pl.program_id(0)
    tiles = [spectrum_ref[pair, :, 0, tile].reshape(N, 128) for pair in range(2) for tile in range(TILES)]
    potential = left_product(rows_ref, jnp.concatenate(tiles, axis=1))
    potential = lane_transform(potential, even_ref, odd_ref)
    prefactor = -1.0 / math.sqrt(N * 8)
    weight = jnp.where(step % 2 == 0, prefactor, 2.0 * prefactor)

    def term(band_ref):
        one = band_ref[:, 0].reshape(N, LANES) * potential[:, :LANES]
        return weight * (one + band_ref[:, 1].reshape(N, LANES) * potential[:, LANES:])

    @pl.when(step == 0)
    def _():
        total_ref[...] = term(first_ref)

    @pl.when(step == 1)
    def _():
        total_ref[...] += term(first_ref)

    @pl.when(step >= 2)
    def _():
        total_ref[...] += term(last_ref)

    @pl.when(step == 3)
    def _():
        for z in range(8):
            for source in range(4):
                rows = pl.ds(24 * z + 6 * source, 6)
                for tile in range(TILES):
                    block = total_ref[rows, 128 * tile : 128 * tile + 128]
                    out_ref[z, 56 * source + 6 * tile : 56 * source + 6 * tile + 6, :] = block


def unpack_kernel(blocks_ref, out_ref, left_ref, right_ref):
    source = blocks_ref.reshape(32 * 56, 128)
    lower = lax.broadcasted_iota(jnp.int32, (32, 128), 1) < 64
    for a in range(6):
        left, right = left_ref.at[a % 2], right_ref.at[a % 2]
        for h in range(3):
            tiles = [source[pl.ds(18 * h + 6 * k + a, 32, stride=56), :] for k in range(3)]
            even, odd = pl.ds(2 * h, 32, stride=6), pl.ds(2 * h + 1, 32, stride=6)
            turned = pltpu.roll(tiles[2], 64, 1)
            left[even, :] = tiles[0]
            right[even, :] = tiles[1]
            left[odd, :] = jnp.where(lower, pltpu.roll(tiles[1], 64, 1), turned)
            right[odd, :] = turned
        out_ref[0, a, :, :128] = left[...]
        out_ref[0, a, :, 128:] = right[:, :64]


def filter_block(columns_ref, pair_ref, wave_ref, to_ref, from_ref, out_ref):
    source = columns_ref.reshape(32 * TILES * 8, 128)
    target = out_ref.reshape(32 * TILES * 8, 128)
    lower = lax.broadcasted_iota(jnp.int32, (32, 128), 1) < 64

    def rows(tile, k):
        return pl.ds(8 * tile + k, 32, stride=TILES * 8)

    blocks = []
    for k in range(8):
        tiles = [3 * (i // 2) + 2 * (i % 2) for i in range(6)]
        blocks.append(jnp.concatenate([source[rows(tile, k), :] for tile in tiles], axis=0))
    for k in range(0, 8, 2):
        parts = []
        for tile in (1, 4, 7):
            one, two = source[rows(tile, k), :], source[rows(tile, k + 1), :]
            parts.append(jnp.where(lower, one, pltpu.roll(two, 64, 1)))
            parts.append(jnp.where(lower, pltpu.roll(one, 64, 1), two))
        blocks.append(jnp.concatenate(parts, axis=0))
    columns = jnp.concatenate(blocks, axis=1)
    spectrum = left_product(to_ref, columns)
    spectrum = spectrum * ((4.0 * math.pi / float(N) ** 3) / (wave_ref[...] + pair_ref[0]))
    columns = left_product(from_ref, spectrum)
    for k in range(8):
        for i in range(6):
            tile = 3 * (i // 2) + 2 * (i % 2)
            target[rows(tile, k), :] = columns[32 * i : 32 * i + 32, 128 * k : 128 * k + 128]
    for k in range(0, 8, 2):
        start = 1024 + 64 * k
        for h in range(3):
            one = columns[64 * h : 64 * h + 32, start : start + 128]
            two = columns[64 * h + 32 : 64 * h + 64, start : start + 128]
            target[rows(3 * h + 1, k), :] = jnp.where(lower, one, pltpu.roll(two, 64, 1))
            target[rows(3 * h + 1, k + 1), :] = jnp.where(lower, pltpu.roll(one, 64, 1), two)


def filter_kernel(first_ref, last_ref, *refs):
    step = pl.program_id(0)

    @pl.when(step < 3)
    def _():
        filter_block(first_ref, *refs)

    @pl.when(step >= 3)
    def _():
        filter_block(last_ref, *refs)


def whole(array):
    return pl.BlockSpec(array.shape, lambda step: (0,) * len(array.shape))


PARAMS = pltpu.CompilerParams(vmem_limit_bytes=VMEM)
COST = pl.CostEstimate(flops=16 * 10**9, bytes_accessed=10**7, transcendentals=0)
BANDS = pl.BlockSpec((8, 2, 24, LANES), lambda step: (0, step, 0, 0))
SPECTRA = pl.BlockSpec((2, 8, TILES, 24, 128), lambda step: (step, 0, 0, 0, 0))


MOVES = pltpu.CompilerParams(vmem_limit_bytes=16 * 1024 * 1024)
MOVED = pl.CostEstimate(flops=0, bytes_accessed=4 * 10**6, transcendentals=0)


def to_blocks(planes, count, part):
    return pl.pallas_call(
        pack_kernel,
        grid=(1,),
        in_specs=[pl.BlockSpec((count, 6, N, N), lambda step: (part, 0, 0, 0))],
        out_specs=pl.BlockSpec((32, 56 * count, 128), lambda step: (0, 0, 0)),
        out_shape=jax.ShapeDtypeStruct((32, 56 * count, 128), jnp.float32),
        scratch_shapes=[pltpu.VMEM((2, N, 128), jnp.float32)] * 2,
        compiler_params=PARAMS,
        cost_estimate=MOVED,
        name="pack",
    )(planes)


def from_blocks(blocks):
    return pl.pallas_call(
        unpack_kernel,
        out_shape=jax.ShapeDtypeStruct((1, 6, N, N), jnp.float32),
        scratch_shapes=[pltpu.VMEM((2, N, 128), jnp.float32)] * 2,
        compiler_params=MOVES,
        cost_estimate=MOVED,
        name="unpack",
    )(blocks)


def by_slots(slots, spread):
    return pl.pallas_call(
        slots_kernel,
        in_specs=[pl.BlockSpec(memory_space=pltpu.SMEM), pl.BlockSpec(memory_space=pltpu.VMEM)],
        out_specs=[pl.BlockSpec(memory_space=pltpu.VMEM)] * 8,
        out_shape=[jax.ShapeDtypeStruct((24, LANES), jnp.float32)] * 8,
        compiler_params=MOVES,
        cost_estimate=MOVED,
        name="slots",
    )(slots, spread)


def choose(owner, spread):
    return pl.pallas_call(
        choose_kernel,
        grid_spec=pltpu.PrefetchScalarGridSpec(
            num_scalar_prefetch=1,
            grid=(2,),
            in_specs=[pl.BlockSpec((1, 4, 112, 128), lambda turn, owner: (owner[turn], 0, 0, 0))],
            out_specs=pl.BlockSpec((2, 24, LANES), lambda turn, owner: (turn, 0, 0)),
        ),
        out_shape=jax.ShapeDtypeStruct((4, 24, LANES), jnp.float32),
        compiler_params=MOVES,
        cost_estimate=MOVED,
        name="choose",
    )(owner, spread)


def forward(slots, pieces, bands):
    even, odd = lane_matrices()
    even, odd = lane_terms(even), lane_terms(odd)
    rows = stacked_terms(cas_matrix()[:, held_order()])
    return pl.pallas_call(
        forward_kernel,
        grid=(2,),
        in_specs=[
            pl.BlockSpec(memory_space=pltpu.SMEM),
            *[whole(piece) for piece in pieces],
            BANDS,
            whole(even),
            whole(odd),
            whole(rows),
        ],
        out_specs=SPECTRA,
        out_shape=jax.ShapeDtypeStruct((4, 8, TILES, 24, 128), jnp.float32),
        scratch_shapes=[pltpu.VMEM((8, 24, LANES), jnp.float32)],
        compiler_params=PARAMS,
        cost_estimate=COST,
        name="forward",
    )(slots, *pieces, bands, even, odd, rows)


def inverse(spectra, bands):
    even, odd = lane_matrices()
    even, odd = lane_terms(even), lane_terms(odd.T)
    rows = stacked_terms(cas_matrix()[held_order(), :])
    out = jax.ShapeDtypeStruct((8, 224, 128), jnp.float32)
    return pl.pallas_call(
        inverse_kernel,
        grid=(4,),
        in_specs=[
            pl.BlockSpec((2, 8, 1, TILES, 24, 128), lambda step: (step % 2, 0, step // 2, 0, 0, 0)),
            pl.BlockSpec((8, 2, 24, LANES), lambda step: (0, jnp.minimum(step, 1), 0, 0)),
            pl.BlockSpec((8, 2, 24, LANES), lambda step: (0, jnp.maximum(step - 2, 0), 0, 0)),
            whole(even),
            whole(odd),
            whole(rows),
        ],
        out_specs=whole(out),
        out_shape=out,
        scratch_shapes=[pltpu.VMEM((N, LANES), jnp.float32)],
        compiler_params=pltpu.CompilerParams(vmem_limit_bytes=32 * 1024 * 1024),
        cost_estimate=COST,
        name="inverse",
    )(spectra, *bands, even, odd, rows)


def filtered(first, last, pair_wave, wave):
    to = stacked_terms(cas_matrix()[:, column_order()])
    back = stacked_terms(cas_matrix()[column_order(), :])
    block = (32, TILES, 8, 128)
    return pl.pallas_call(
        filter_kernel,
        grid=(6,),
        in_specs=[
            pl.BlockSpec(block, lambda step: (0, 0, jnp.minimum(step, 2), 0)),
            pl.BlockSpec(block, lambda step: (0, 0, jnp.maximum(step - 3, 0), 0)),
            pl.BlockSpec((1, 1, 8 * N), lambda step: (step % 3, 0, 0)),
            whole(wave),
            whole(to),
            whole(back),
        ],
        out_specs=pl.BlockSpec((32, 1, TILES, 8, 128), lambda step: (0, step // 3, 0, step % 3, 0)),
        out_shape=jax.ShapeDtypeStruct((32, 2, TILES, 24, 128), jnp.float32),
        compiler_params=pltpu.CompilerParams(vmem_limit_bytes=32 * 1024 * 1024),
        cost_estimate=COST,
        name="filter",
    )(first, last, pair_wave, wave, to, back)


def wavenumber(index):
    folded = jnp.minimum(index, N - index)
    return folded.astype(jnp.float32) * (2.0 * math.pi / N)


def filter_waves(place):
    wave = wavenumber(jnp.arange(N, dtype=jnp.int32)) ** 2
    mine = wavenumber((place % 8) * 24 + jnp.arange(24, dtype=jnp.int32)) ** 2
    screen = (4.0 * math.pi / N) ** 2
    pair = mine.reshape(3, 8, 1) + wave[None, None, :] + screen
    pair = jnp.concatenate([pair[:, :, :128].reshape(3, 1024), pair[:, :, 128:].reshape(3, 512)], axis=1)
    return pair.reshape(3, 1, 8 * N), wave.reshape(N, 1)


def exchange_plane(blocks):
    return lax.all_to_all(blocks, PLANE, 0, 0, tiled=True)


def exchange_z(blocks):
    return lax.all_to_all(blocks, "z", 0, 0, tiled=True)


SHIFTS = (0, 4, 3, 5, 2, 6, 1, 7)


def gather_orbital(spread, place):
    shifts = jnp.array(SHIFTS, jnp.int32)
    pieces = by_slots((place + shifts) % 8, spread)
    moved = [
        lax.ppermute(piece, "z", [(z, (z + shift) % 8) for z in range(8)])
        for piece, shift in zip(pieces[1:], SHIFTS[1:])
    ]
    return [pieces[0]] + moved, (place - shifts) % 8


def shards(resident, owned, owner):
    pair_wave, wave = filter_waves(lax.axis_index(PLANE))
    first = exchange_plane(to_blocks(owned[0], 2, 0))
    spread, first = lax.optimization_barrier((to_blocks(resident, 1, 0), first))
    halves = [lax.all_gather(choose(owner, first.reshape(8, 4, 112, 128)), "z", axis=0, tiled=False)]
    spread = exchange_plane(spread)
    second, spread = lax.optimization_barrier((to_blocks(owned[0], 2, 1), spread))
    orbital, slots = gather_orbital(spread.reshape(8, 4, 56, 128), lax.axis_index("z"))
    second, orbital = lax.optimization_barrier((exchange_plane(second), orbital))
    second = choose(owner, second.reshape(8, 4, 112, 128))
    halves.append(lax.all_gather(second, "z", axis=0, tiled=False))
    spectra = []
    for bands in halves:
        blocks = forward(slots, orbital, bands)
        blocks, pair_wave, wave = lax.optimization_barrier((blocks, pair_wave, wave))
        spectra.append(exchange_plane(blocks.reshape(32, 216, 128)).reshape(32, TILES, 24, 128))
    potentials = exchange_plane(filtered(*spectra, pair_wave, wave).reshape(32, 432, 128))
    total = inverse(potentials.reshape(4, 8, 2, TILES, 24, 128), halves)
    back = exchange_plane(exchange_z(total).reshape(32, 56, 128))
    return from_blocks(back)


def solution(mesh):
    fine = Mesh(mesh.devices.reshape(2, 4, 2, 8, 2), ("x_lo", "y", "x_hi", "z", "core"))
    band, slab = ("x_lo", "y"), ("x_hi", "z", "core")
    return jax.shard_map(
        shards,
        mesh=fine,
        in_specs=(P(band, slab), P(band, None, slab), P()),
        out_specs=P(band, slab),
        check_vma=False,
    )
```
